256 devices in a mesh: row: 8 (over z_hi, x), col: 16 (over z_lo, y), chan: 2 (over core).
Axes of the slice: x: 4, y: 4, z: 8 (z_hi: 2, z_lo: 4; z = z_hi * 4 + z_lo), core: 2. Of those that a mesh axis runs over, the one named last changes fastest.
Arguments:
- image: bfloat16 [192, 512, 2048], P('chan', 'row', 'col'), may hold values from -6 to 6
- kernel_one: float32 [192, 7, 7], P('chan'), may hold values from -0.875 to 0.875
- kbias_one: float32 [192], P('chan'), may hold values from -3 to 3
- gain_one: float32 [192], replicated, may hold values from 0.1 to 1.9
- shift_one: float32 [192], replicated, may hold values from -3 to 3
- expand_one: bfloat16 [192, 768], P(None, 'chan'), may hold values from -0.4375 to 0.4375
- ebias_one: float32 [768], P('chan'), may hold values from -3 to 3
- reduce_one: bfloat16 [768, 192], P('chan'), may hold values from -0.21875 to 0.21875
- rbias_one: float32 [192], replicated, may hold values from -3 to 3
- scale_one: float32 [192], replicated, may hold values from 0.3 to 1
- pool_gain: float32 [192], replicated, may hold values from 0.1 to 1.9
- pool_shift: float32 [192], replicated, may hold values from -3 to 3
- pool_weight: bfloat16 [4, 192, 384], P(None, None, 'chan'), may hold values from -0.21875 to 0.21875
- pool_bias: float32 [384], P('chan'), may hold values from -3 to 3
- kernel_two: float32 [384, 7, 7], P('chan'), may hold values from -0.875 to 0.875
- kbias_two: float32 [384], P('chan'), may hold values from -3 to 3
- gain_two: float32 [384], replicated, may hold values from 0.1 to 1.9
- shift_two: float32 [384], replicated, may hold values from -3 to 3
- expand_two: bfloat16 [384, 1536], P(None, 'chan'), may hold values from -0.3125 to 0.3125
- ebias_two: float32 [1536], P('chan'), may hold values from -3 to 3
- reduce_two: bfloat16 [1536, 384], P('chan'), may hold values from -0.15625 to 0.15625
- rbias_two: float32 [384], replicated, may hold values from -3 to 3
- scale_two: float32 [384], replicated, may hold values from 0.3 to 1
Outputs:
- block_one: bfloat16 [192, 512, 2048], P('chan', 'row', 'col')
- block_two: bfloat16 [384, 256, 1024], P('chan', 'row', 'col')
The draws below stay inside these ranges and needn't reach their ends.
All inputs are finite; a program needn't handle non-finite values.
Results may differ from the reference program's by a relative error of at most 0.017.
Values may be sent and summed in bfloat16 or wider, within the bound.
No kernel may reach another device: no remote copies, remote signals or barrier semaphores. Data moves between devices by JAX's collectives and lax.ppermute only.
A program may use at most 128 MiB of HBM per device.

```python
import math
import jax
import jax.numpy as jnp
from jax import lax

C1 = 192
HID1 = 768
C2 = 384
HID2 = 1536
H = 512
W = 2048
N_ROW = 8


def level_of(own_key, extent, split, low, largest):
    level, own = 1.0, jax.random.fold_in(own_key, 6)
    for dim, parts in split:
        draws = jnp.exp(jax.random.uniform(jax.random.fold_in(own, dim), (parts,), jnp.float32, low / len(split), largest / len(split)))
        level = level * jnp.repeat(draws, extent[dim] // parts).reshape([-1 if axis == dim else 1 for axis in range(len(extent))])
    return level


def normal_values(own_key, dims, scale, limit, split=(), kind=jnp.bfloat16):
    values = scale * jax.random.normal(own_key, dims, jnp.float32)
    if split:
        values = values * level_of(own_key, dims, split, -0.22, 0.18)
    return jnp.clip(values, -limit, limit).astype(kind)


def setup_inputs(seed: int = 0) -> dict:
    key_list = jax.random.split(jax.random.key(seed), 24)
    return {
        "image": normal_values(key_list[0], (C1, H, W), 1.0, 6.0, ((0, 2), (1, 8), (2, 16))),
        "kernel_one": normal_values(key_list[1], (C1, 7, 7), 49 ** -0.5, 0.875, ((0, 2),), jnp.float32),
        "kbias_one": normal_values(key_list[2], (C1,), 0.5, 3.0, ((0, 2),), jnp.float32),
        "gain_one": jnp.clip(1.0 + 0.18 * jax.random.normal(key_list[3], (C1,), jnp.float32), 0.1, 1.9),
        "shift_one": normal_values(key_list[4], (C1,), 0.5, 3.0, (), jnp.float32),
        "expand_one": normal_values(key_list[5], (C1, HID1), C1 ** -0.5, 0.4375, ((1, 2),)),
        "ebias_one": normal_values(key_list[6], (HID1,), 0.5, 3.0, ((0, 2),), jnp.float32),
        "reduce_one": normal_values(key_list[7], (HID1, C1), HID1 ** -0.5, 0.21875, ((0, 2),)),
        "rbias_one": normal_values(key_list[8], (C1,), 0.5, 3.0, (), jnp.float32),
        "scale_one": jnp.clip(jnp.exp(jax.random.uniform(key_list[9], (C1,), jnp.float32, math.log(0.3), math.log(1.0))), 0.3, 1.0),
        "pool_gain": jnp.clip(1.0 + 0.18 * jax.random.normal(key_list[10], (C1,), jnp.float32), 0.1, 1.9),
        "pool_shift": normal_values(key_list[11], (C1,), 0.5, 3.0, (), jnp.float32),
        "pool_weight": normal_values(key_list[12], (4, C1, C2), (4 * C1) ** -0.5, 0.21875, ((2, 2),)),
        "pool_bias": normal_values(key_list[13], (C2,), 0.5, 3.0, ((0, 2),), jnp.float32),
        "kernel_two": normal_values(key_list[14], (C2, 7, 7), 49 ** -0.5, 0.875, ((0, 2),), jnp.float32),
        "kbias_two": normal_values(key_list[15], (C2,), 0.5, 3.0, ((0, 2),), jnp.float32),
        "gain_two": jnp.clip(1.0 + 0.18 * jax.random.normal(key_list[16], (C2,), jnp.float32), 0.1, 1.9),
        "shift_two": normal_values(key_list[17], (C2,), 0.5, 3.0, (), jnp.float32),
        "expand_two": normal_values(key_list[18], (C2, HID2), C2 ** -0.5, 0.3125, ((1, 2),)),
        "ebias_two": normal_values(key_list[19], (HID2,), 0.5, 3.0, ((0, 2),), jnp.float32),
        "reduce_two": normal_values(key_list[20], (HID2, C2), HID2 ** -0.5, 0.15625, ((0, 2),)),
        "rbias_two": normal_values(key_list[21], (C2,), 0.5, 3.0, (), jnp.float32),
        "scale_two": jnp.clip(jnp.exp(jax.random.uniform(key_list[22], (C2,), jnp.float32, math.log(0.3), math.log(1.0))), 0.3, 1.0),
    }


def depthwise(padded, kernel, kbias, rows, cols):
    total = jnp.zeros((padded.shape[0], rows, cols), jnp.float32)
    for first in range(7):
        for second in range(7):
            window = padded[:, first:first + rows, second:second + cols].astype(jnp.float32)
            total = total + window * kernel[:, first, second][:, None, None]
    return total + kbias[:, None, None]

def channel_norm(values, gain, shift):
    center = values - lax.optimization_barrier(jnp.mean(values, axis=0, keepdims=True))
    spread = lax.optimization_barrier(jnp.mean(center * center, axis=0, keepdims=True))
    return center * lax.rsqrt(spread + 1e-06) * gain[:, None, None] + shift[:, None, None]

def pointwise(normed, expand, ebias, reduce_value, rbias, scale, base):
    width = normed.shape[0]
    flat = normed.reshape(width, -1)
    hidden = jax.nn.gelu(jnp.dot(expand.T, flat, preferred_element_type=jnp.float32) + ebias[:, None], approximate=False).astype(jnp.bfloat16)
    summed = jnp.dot(reduce_value.T, hidden, preferred_element_type=jnp.float32)
    result = base.reshape(width, -1).astype(jnp.float32) + scale[:, None] * (summed + rbias[:, None])
    return result.astype(jnp.bfloat16).reshape(base.shape)

def split_rows(array, count):
    width, rows, cols = array.shape
    return array.reshape(width, count, rows // count, cols).transpose(1, 0, 2, 3)

def join_rows(array):
    count, width, rows, cols = array.shape
    return array.transpose(1, 0, 2, 3).reshape(width, count * rows, cols)

def reference(image, kernel_one, kbias_one, gain_one, shift_one, expand_one, ebias_one, reduce_one, rbias_one, scale_one, pool_gain, pool_shift, pool_weight, pool_bias, kernel_two, kbias_two, gain_two, shift_two, expand_two, ebias_two, reduce_two, rbias_two, scale_two):
    rows, cols = (image.shape[1], image.shape[2])
    padded = jnp.pad(image, ((0, 0), (3, 3), (3, 3)))
    mixed_one = depthwise(padded, kernel_one, kbias_one, rows, cols).astype(jnp.bfloat16)

    def section_one(pair):
        mixed, base = pair
        normed = channel_norm(mixed.astype(jnp.float32), gain_one, shift_one).astype(jnp.bfloat16)
        block = pointwise(normed, expand_one, ebias_one, reduce_one, rbias_one, scale_one, base)
        pnorm = channel_norm(block.astype(jnp.float32), pool_gain, pool_shift).astype(jnp.bfloat16)
        half_rows, half_cols = (block.shape[1] // 2, block.shape[2] // 2)
        quads = pnorm.reshape(block.shape[0], half_rows, 2, half_cols, 2)
        total = jnp.zeros((pool_weight.shape[2], half_rows * half_cols), jnp.float32)
        for down in range(2):
            for right in range(2):
                sub = quads[:, :, down, :, right].reshape(block.shape[0], -1)
                total = total + jnp.dot(pool_weight[2 * down + right].T, sub, preferred_element_type=jnp.float32)
        pooled = (total + pool_bias[:, None]).astype(jnp.bfloat16).reshape(-1, half_rows, half_cols)
        return (block, pooled)
    blocks, pools = lax.map(section_one, (split_rows(mixed_one, N_ROW), split_rows(image, N_ROW)))
    block_one = join_rows(blocks)
    pooled = join_rows(pools)
    coarse_rows, coarse_cols = (pooled.shape[1], pooled.shape[2])
    padded_two = jnp.pad(pooled, ((0, 0), (3, 3), (3, 3)))
    mixed_two = depthwise(padded_two, kernel_two, kbias_two, coarse_rows, coarse_cols).astype(jnp.bfloat16)

    def section_two(pair):
        mixed, base = pair
        normed = channel_norm(mixed.astype(jnp.float32), gain_two, shift_two).astype(jnp.bfloat16)
        return pointwise(normed, expand_two, ebias_two, reduce_two, rbias_two, scale_two, base)
    block_two = join_rows(lax.map(section_two, (split_rows(mixed_two, N_ROW), split_rows(pooled, N_ROW))))
    return (block_one, block_two)
```

```python
import functools

import jax
import jax.numpy as jnp
from jax import lax
from jax.experimental import pallas as pl
from jax.experimental.pallas import tpu as pltpu
from jax.sharding import PartitionSpec as P

F32 = jnp.float32
BF16 = jnp.bfloat16
LANES = 128
SIDE = 3
TAPS = 7
VMEM_LIMIT = 56 << 20


def call(body, outs, scratch=(), flops=0, moved=0, name=None):
    return pl.pallas_call(
        body,
        out_shape=tuple(jax.ShapeDtypeStruct(shape, kind) for shape, kind in outs),
        scratch_shapes=list(scratch),
        compiler_params=pltpu.CompilerParams(vmem_limit_bytes=VMEM_LIMIT),
        cost_estimate=pl.CostEstimate(flops=flops, bytes_accessed=moved, transcendentals=0),
        name=name,
    )


def lane_of(shape):
    return lax.broadcasted_iota(jnp.int32, shape, 1)


def turn(values, amount):
    return pltpu.roll(values, amount % LANES, 1)


def weights_body(expand_one, reduce_one, pool, expand_two, reduce_two, first, second):
    hid_one, wide_one = (expand_one.shape[1], expand_one.shape[0])
    first[0:hid_one, 0:wide_one] = expand_one[...].T
    first[hid_one : hid_one + wide_one, :] = reduce_one[...].T
    base = hid_one + wide_one
    for quad in range(4):
        first[base + wide_one * quad : base + wide_one * (quad + 1), 0:wide_one] = pool[quad].T
    hid_two, wide_two = (expand_two.shape[1], expand_two.shape[0])
    second[0:hid_two, :] = expand_two[...].T
    for part in range(2):
        second[hid_two + wide_two * part : hid_two + wide_two * (part + 1), :] = reduce_two[
            wide_two * part : wide_two * (part + 1), :
        ].T


def pack_rows(read, places, group, left_out, right_out, channels):
    width = LANES // group
    for start in range(0, channels, 32):
        part = pl.ds(start, 32)
        lane = lane_of((32, LANES))
        left = jnp.zeros((32, LANES), F32)
        right = jnp.zeros((32, LANES), F32)
        for row, first, packed in places:
            values = read(row, part)
            inside = (lane >= SIDE * packed) & (lane < SIDE * packed + SIDE)
            left = jnp.where(inside, turn(values, SIDE * packed - first), left)
            last = first + width - SIDE
            right = jnp.where(inside, turn(values, SIDE * packed - last), right)
        left_out[part, :] = left.astype(BF16)
        right_out[part, :] = right.astype(BF16)


def assemble_one_body(own, sib, outer, whole, left_out, right_out):
    half = lax.axis_index("chan")
    count, group = (own.shape[0], own.shape[1])
    mine = pl.ds(pl.multiple_of(half * group, 16), group)
    other = pl.ds(pl.multiple_of((1 - half) * group, 16), group)
    rows = pl.ds(SIDE * (1 - half), count)
    edge = pl.ds(count * half, SIDE)
    whole[rows, mine, :] = own[...]
    whole[rows, other, :] = sib[...]
    whole[edge, other, :] = outer[:, 0:group, :]
    whole[edge, mine, :] = outer[:, group:, :]
    places = [(row, 0, row) for row in range(whole.shape[0])]
    pack_rows(lambda r, c: whole[r, c, :].astype(F32), places, 1, left_out, right_out, 2 * group)


def assemble_two_body(pooled, from_sib, from_outer, whole, left_out, right_out):
    top_is_outer = lax.axis_index("chan") == 0
    count, channels = (pooled.shape[0], pooled.shape[1])
    for row in range(count):
        whole[SIDE + row] = pooled[row]
    for start in range(0, channels, 64):
        part = pl.ds(start, 64)
        low = lane_of((64, LANES)) < LANES // 2

        def get(ref, row):
            return ref[row, part, :].astype(F32)

        sib0, sib1 = (get(from_sib, 0), get(from_sib, 1))
        out0, out1 = (get(from_outer, 0), get(from_outer, 1))
        top0, top1 = (jnp.where(top_is_outer, out0, sib0), jnp.where(top_is_outer, out1, sib1))
        low0, low1 = (jnp.where(top_is_outer, sib0, out0), jnp.where(top_is_outer, sib1, out1))
        above = (top0, turn(top0, 64), top1)
        below = (turn(low0, 64), low0, turn(low1, 64))
        for k in range(SIDE):
            mid = turn(get(pooled, count - SIDE + k), 64)
            whole[k, part, :] = jnp.where(low, above[k], mid).astype(BF16)
            mid = turn(get(pooled, k), 64)
            whole[SIDE + count + k, part, :] = jnp.where(low, mid, below[k]).astype(BF16)
    rows = count + 2 * SIDE
    places = [(k, 0, k) for k in range(rows)]
    places += [(k, 64, k + count) for k in range(rows - count, rows)]
    pack_rows(lambda r, c: whole[r, c, :].astype(F32), places, 2, left_out, right_out, channels)


def conv_body(whole, small_own, small_sib, out, taps, kbias):
    half = lax.axis_index("chan")
    rows, channels = (out.shape[0], out.shape[1])
    group = channels // 2
    for place, ref in ((half, small_own), (1 - half, small_sib)):
        part = pl.ds(pl.multiple_of(place * group, 16), group)
        columns = ref[...]
        for tap in range(TAPS * TAPS):
            taps[tap, part, :] = jnp.broadcast_to(
                columns[:, tap : tap + 1], (group, LANES)
            ).astype(BF16)
        kbias[part, :] = jnp.broadcast_to(
            columns[:, TAPS * TAPS : TAPS * TAPS + 1], (group, LANES)
        )
    blocks = channels // 16
    high = 8

    def step(index, carry):
        part = pl.ds(pl.multiple_of(lax.rem(index, blocks) * 16, 16), 16)
        start = lax.div(index, blocks) * high
        read = [whole[start + k, part, :] for k in range(high + TAPS - 1)]
        totals = [kbias[part, :] for _ in range(high)]
        for second in range(TAPS):
            column = [taps[TAPS * first + second, part, :] for first in range(TAPS)]
            for k in range(high):
                terms = [read[k + first] * column[first] for first in range(TAPS)]
                total = terms[0]
                for term in terms[1:]:
                    total = total + term
                total = total.astype(F32)
                if second != SIDE:
                    total = turn(total, SIDE - second)
                totals[k] = totals[k] + total
        for k in range(high):
            out[start + k, part, :] = totals[k].astype(BF16)
        return carry

    lax.fori_loop(0, blocks * (rows // high), step, 0)


def side_sums(left_in, right_in, left_own, right_own, small_own, small_sib, group, sums):
    half = lax.axis_index("chan")
    channels = left_in.shape[0]
    count = channels // 2
    for place, ref in ((half, small_own), (1 - half, small_sib)):
        part = pl.ds(pl.multiple_of(place * count, 16), count)
        lane = lane_of((count, LANES))
        column = lax.rem(lane, SIDE) if group == 1 else lax.rem(lax.rem(lane, 64), SIDE)
        pairs = ((left_in, right_own), (right_in, left_own))
        for side, (came, wrapped) in enumerate(pairs):
            fresh, stale = (came[part, :].astype(F32), wrapped[part, :].astype(F32))
            if group == 1:
                outside = fresh - stale
            else:
                upper = fresh - turn(stale, -24)
                lower = turn(turn(fresh, -24) - stale, 64)
                outside = jnp.where(lane < 64, upper, lower)
            total = jnp.zeros((count, LANES), F32)
            for near in range(SIDE):
                second = near if side == 0 else near + 4
                source = near if side == 0 else second - 6
                keep = (column + source >= 0) & (column + source < SIDE)
                partial = jnp.zeros((count, LANES), F32)
                for first in range(TAPS):
                    tap = TAPS * first + second
                    weight = ref[:, tap : tap + 1]
                    partial = partial + weight * turn(outside, -(SIDE * first + source))
                total = total + jnp.where(keep, partial, 0.0)
            sums[side, part, :] = total


def with_sides(mixed, sums, row, group):
    width = LANES // group
    lane = lane_of(mixed.shape)
    column = lane if group == 1 else lax.rem(lane, width)
    first = pltpu.roll(sums[0], LANES - SIDE * row, 1)
    last = pltpu.roll(sums[1], width - SIDE + (0 if group == 1 else LANES) - SIDE * row, 1)
    mixed = mixed + jnp.where(column < SIDE, first, 0.0)
    return mixed + jnp.where(column >= width - SIDE, last, 0.0)


def channel_norm(values, gain, shift):
    center = values - jnp.mean(values, axis=0, keepdims=True)
    spread = jnp.mean(center * center, axis=0, keepdims=True)
    return center * (lax.rsqrt(spread + 1e-06)) * gain + shift


def gelu(values):
    return 0.5 * values * (1.0 + lax.erf(values * 0.7071067811865476))


def dot(a, b):
    return jnp.dot(a, b, preferred_element_type=F32)


def bias_columns(ref, at, out, base):
    count = ref.shape[0]
    for k in range(4):
        out[base + count * k : base + count * (k + 1), :] = ref[:, at + k : at + k + 1]


def section_one_body(
    conv, whole, left_in, right_in, left_own, right_own, small_own, small_sib, vectors,
    weights_own, weights_sib, pbias_own, pbias_sib,
    out_own, out_sib, pooled, to_sib, to_outer,
    sums, quads, ebias,
):
    half = lax.axis_index("chan")
    rows, channels = (conv.shape[0], conv.shape[1])
    group = channels // 2
    hidden = weights_own.shape[1]
    side_sums(left_in, right_in, left_own, right_own, small_own, small_sib, 1, sums)
    bias_columns(small_own, TAPS * TAPS + 1, ebias, 0)
    bias_columns(small_sib, TAPS * TAPS + 1, ebias, hidden)
    even = lax.broadcasted_iota(jnp.int32, (2 * LANES, 2 * LANES), 0)
    to = lax.broadcasted_iota(jnp.int32, (2 * LANES, 2 * LANES), 1)
    source = 2 * lax.rem(to, LANES) + lax.div(to, LANES)
    pick = jnp.where(even == source, 1.0, 0.0).astype(BF16)
    lane = lane_of((channels, LANES))
    first_rows = rows // 2

    def step(index, carry):
        order = [2 * index, 2 * index + first_rows, 2 * index + 1, 2 * index + 1 + first_rows]
        gain, shift, rbias, scale = (vectors[:, k : k + 1] for k in range(4))
        pgain, pshift = (vectors[:, 4:5], vectors[:, 5:6])
        mixed = jnp.concatenate(
            [with_sides(conv[row].astype(F32), sums, row, 1) for row in order], axis=1
        )
        normed = channel_norm(mixed, gain, shift).astype(BF16)
        summed = None
        for place, ref in enumerate((weights_own, weights_sib)):
            inner = dot(ref[0:hidden, 0:channels], normed)
            inner = gelu(inner + ebias[hidden * place : hidden * (place + 1), :]).astype(BF16)
            term = dot(ref[hidden : hidden + channels, :], inner)
            summed = term if summed is None else summed + term
        base = jnp.concatenate([whole[row + SIDE].astype(F32) for row in order], axis=1)
        block = (base + scale * (summed + rbias)).astype(BF16)
        for k, row in enumerate(order):
            low = block[0:group, LANES * k : LANES * (k + 1)]
            top = block[group:, LANES * k : LANES * (k + 1)]
            out_own[row] = jnp.where(half == 0, low, top)
            out_sib[row] = jnp.where(half == 0, top, low)
        pnorm = channel_norm(block.astype(F32), pgain, pshift).astype(BF16)
        for down in range(2):
            parted = dot(pnorm[:, 2 * LANES * down : 2 * LANES * (down + 1)], pick).astype(BF16)
            at = pl.ds(pl.multiple_of(index * LANES, LANES), LANES)
            quads[2 * down, :, at] = parted[:, 0:LANES]
            quads[2 * down + 1, :, at] = parted[:, LANES:]
        return carry

    lax.fori_loop(0, rows // 4, step, 0)
    base = hidden + channels
    for place, ref, bias in ((half, weights_own, pbias_own), (1 - half, weights_sib, pbias_sib)):
        total = None
        for quad in range(4):
            term = dot(
                ref[base + channels * quad : base + channels * (quad + 1), 0:channels], quads[quad]
            )
            total = term if total is None else total + term
        total = (total + bias[...]).astype(BF16)
        part = pl.ds(pl.multiple_of(place * channels, 16), channels)
        for row in range(pooled.shape[0]):
            pooled[row, part, :] = total[:, LANES * row : LANES * (row + 1)]
    count = pooled.shape[0]
    for start in range(0, pooled.shape[1], 64):
        part = pl.ds(start, 64)
        low = lane_of((64, LANES)) < 64
        read = {k: pooled[k, part, :].astype(F32) for k in (0, 1, 2, count - 3, count - 2, count - 1)}
        top = (jnp.where(low, read[0], turn(read[1], 64)), read[2])
        bottom = (
            jnp.where(low, turn(read[count - 3], 64), read[count - 2]),
            turn(read[count - 1], 64),
        )
        for k in range(2):
            to_sib[k, part, :] = jnp.where(half == 0, bottom[k], top[k]).astype(BF16)
            to_outer[k, part, :] = jnp.where(half == 0, top[k], bottom[k]).astype(BF16)


def section_two_body(
    conv, whole, left_in, right_in, left_own, right_own, small_own, small_sib, vectors,
    weights_own, weights_sib,
    out_own, out_sib,
    sums, ebias,
):
    half = lax.axis_index("chan")
    rows, channels = (conv.shape[0], conv.shape[1])
    group = channels // 2
    hidden = 2 * channels
    side_sums(left_in, right_in, left_own, right_own, small_own, small_sib, 2, sums)
    bias_columns(small_own, TAPS * TAPS + 1, ebias, 0)
    bias_columns(small_sib, TAPS * TAPS + 1, ebias, hidden)

    def step(index, carry):
        order = [4 * index + k for k in range(4)]
        gain, shift, rbias, scale = (vectors[:, k : k + 1] for k in range(4))
        mixed = jnp.concatenate(
            [with_sides(conv[row].astype(F32), sums, row, 2) for row in order], axis=1
        )
        normed = channel_norm(mixed, gain, shift).astype(BF16)
        summed = None
        for place, ref in enumerate((weights_own, weights_sib)):
            for part in range(2):
                rows_of = channels * part
                inner = dot(ref[rows_of : rows_of + channels, :], normed)
                at = hidden * place + rows_of
                inner = gelu(inner + ebias[at : at + channels, :]).astype(BF16)
                term = dot(ref[hidden + rows_of : hidden + rows_of + channels, :], inner)
                summed = term if summed is None else summed + term
        base = jnp.concatenate([whole[row + SIDE].astype(F32) for row in order], axis=1)
        block = (base + scale * (summed + rbias)).astype(BF16)
        for k, row in enumerate(order):
            low = block[0:group, LANES * k : LANES * (k + 1)]
            top = block[group:, LANES * k : LANES * (k + 1)]
            out_own[row] = jnp.where(half == 0, low, top)
            out_sib[row] = jnp.where(half == 0, top, low)
        return carry

    lax.fori_loop(0, rows // 4, step, 0)


def on_device(
    image, kernel_one, kbias_one, gain_one, shift_one, expand_one, ebias_one, reduce_one,
    rbias_one, scale_one, pool_gain, pool_shift, pool_weight, pool_bias, kernel_two, kbias_two,
    gain_two, shift_two, expand_two, ebias_two, reduce_two, rbias_two, scale_two,
):
    half = lax.axis_index("chan")
    group, rows, cols = image.shape
    channels = 2 * group
    coarse_group = pool_weight.shape[2]
    coarse = 2 * coarse_group
    half_rows = rows // 2
    packed_rows = half_rows // 4
    n_row, n_col = (lax.axis_size("row"), lax.axis_size("col"))
    swap = [(0, 1), (1, 0)]
    outward = [(2 * r + 1, 2 * r + 2) for r in range(n_row - 1)]
    outward += [(b, a) for a, b in outward]
    right = [(c, c + 1) for c in range(n_col - 1)]
    left = [(b, a) for a, b in right]

    def to_sibling(x):
        return lax.ppermute(x, "chan", swap)

    def to_outer(x):
        return lax.ppermute(x, ("row", "chan"), outward)

    def sides(left_own, right_own):
        return (lax.ppermute(right_own, "col", right), lax.ppermute(left_own, "col", left))

    turned = image.transpose(1, 0, 2)
    span = half_rows + SIDE
    own = lax.dynamic_slice_in_dim(turned, (half_rows - SIDE) * half, span, 0)
    sib = to_sibling(lax.dynamic_slice_in_dim(turned, (half_rows - SIDE) * (1 - half), span, 0))

    first_shape = (expand_one.shape[1] + 5 * channels, expand_one.shape[1])
    second_shape = (2 * expand_two.shape[1], coarse)
    first_own, second_own = call(
        weights_body, [(first_shape, BF16), (second_shape, BF16)], name="turn_weights"
    )(expand_one, reduce_one, pool_weight, expand_two, reduce_two)
    small_one = jnp.concatenate(
        [kernel_one.reshape(group, -1), kbias_one[:, None], ebias_one.reshape(4, group).T], axis=1
    )
    small_two = jnp.concatenate(
        [
            kernel_two.reshape(coarse_group, -1),
            kbias_two[:, None],
            ebias_two.reshape(4, coarse_group).T,
            pool_bias[:, None],
        ],
        axis=1,
    )
    small = jnp.concatenate([jnp.pad(small_one, ((0, 0), (0, 1))), small_two], axis=0)
    small = jnp.pad(small, ((0, 0), (0, LANES - small.shape[1])))
    small_sib = to_sibling(small)
    first_sib = to_sibling(first_own)
    vectors_one = jnp.stack(
        [gain_one, shift_one, rbias_one, scale_one, pool_gain, pool_shift], axis=1
    )
    vectors_two = jnp.stack([gain_two, shift_two, rbias_two, scale_two], axis=1)

    edge = [lax.dynamic_slice_in_dim(x, half_rows * half, SIDE, 0) for x in (own, sib)]
    outer = to_outer(jnp.concatenate(edge, axis=1))
    side_shape = ((channels, LANES), BF16)
    whole, left_own, right_own = call(
        assemble_one_body,
        [((half_rows + 2 * SIDE, channels, LANES), BF16), side_shape, side_shape],
        name="assemble_one",
    )(own, sib, outer)
    left_in, right_in = sides(left_own, right_own)
    one_own, one_sib = (small[:group], small_sib[:group])
    (conv,) = call(
        conv_body,
        [((half_rows, channels, LANES), BF16)],
        [pltpu.VMEM((TAPS * TAPS, channels, LANES), BF16), pltpu.VMEM((channels, LANES), F32)],
        flops=10**10,
        moved=10**7,
        name="conv_one",
    )(whole, one_own, one_sib)
    message = ((2, coarse, LANES), BF16)
    block_shape = ((half_rows, group, LANES), BF16)
    block_own, block_sib, pooled, for_sib, for_outer = call(
        section_one_body,
        [block_shape, block_shape, ((packed_rows, coarse, LANES), BF16), message, message],
        [
            pltpu.VMEM((2, channels, LANES), F32),
            pltpu.VMEM((4, channels, LANES * packed_rows), BF16),
            pltpu.VMEM((2 * expand_one.shape[1], 1), F32),
        ],
        flops=10**10,
        moved=10**7,
        name="section_one",
    )(
        conv, whole, left_in, right_in, left_own, right_own, one_own, one_sib, vectors_one,
        first_own, first_sib, small[group:, 54:55], small_sib[group:, 54:55],
    )
    from_sib = to_sibling(for_sib)
    from_outer = to_outer(for_outer)
    second_sib = to_sibling(second_own)
    side_shape = ((coarse, LANES), BF16)
    whole_two, left_own, right_own = call(
        assemble_two_body,
        [((packed_rows + 2 * SIDE, coarse, LANES), BF16), side_shape, side_shape],
        name="assemble_two",
    )(pooled, from_sib, from_outer)
    left_in, right_in = sides(left_own, right_own)
    block_came = to_sibling(block_sib)
    two_own, two_sib = (small[group:], small_sib[group:])
    (conv,) = call(
        conv_body,
        [((packed_rows, coarse, LANES), BF16)],
        [pltpu.VMEM((TAPS * TAPS, coarse, LANES), BF16), pltpu.VMEM((coarse, LANES), F32)],
        flops=5 * 10**9,
        moved=10**7,
        name="conv_two",
    )(whole_two, two_own, two_sib)
    block_shape = ((packed_rows, coarse_group, LANES), BF16)
    two_block_own, two_block_sib = call(
        section_two_body,
        [block_shape, block_shape],
        [pltpu.VMEM((2, coarse, LANES), F32), pltpu.VMEM((2 * expand_two.shape[1], 1), F32)],
        flops=10**10,
        moved=10**7,
        name="section_two",
    )(
        conv, whole_two, left_in, right_in, left_own, right_own, two_own, two_sib, vectors_two,
        second_own, second_sib,
    )
    two_came = to_sibling(two_block_sib)

    def in_order(mine, came):
        return jnp.where(half == 0, jnp.stack([mine, came]), jnp.stack([came, mine]))

    block_one = in_order(block_own, block_came).reshape(rows, group, cols).transpose(1, 0, 2)
    both = in_order(two_block_own, two_came)
    both = both.reshape(2, packed_rows, coarse_group, 2, cols // 2).transpose(2, 0, 3, 1, 4)
    block_two = both.reshape(coarse_group, half_rows, cols // 2)
    return (block_one, block_two)


def solution(mesh):
    tile = P("chan", "row", "col")
    return jax.shard_map(
        on_device,
        mesh=mesh,
        in_specs=(
            tile, P("chan", None, None), P("chan"), P(), P(), P(None, "chan"), P("chan"),
            P("chan", None), P(), P(), P(), P(), P(None, None, "chan"), P("chan"),
            P("chan", None, None), P("chan"), P(), P(), P(None, "chan"), P("chan"),
            P("chan", None), P(), P(),
        ),
        out_specs=(tile, tile),
        check_vma=False,
    )
```

```python
import functools

import jax
import jax.numpy as jnp
from jax import lax
from jax.experimental import pallas as pl
from jax.experimental.pallas import tpu as pltpu
from jax.sharding import PartitionSpec as P

F32 = jnp.float32
BF16 = jnp.bfloat16
LANES = 128
SIDE = 3
TAPS = 7
VMEM_LIMIT = 56 << 20
LINES = 16


def call(body, outs, scratch=(), flops=0, moved=0, name=None, ins=None):
    return pl.pallas_call(
        body,
        **({} if ins is None else {"grid": (1,), "in_specs": ins}),
        out_shape=tuple(jax.ShapeDtypeStruct(shape, kind) for shape, kind in outs),
        scratch_shapes=list(scratch),
        compiler_params=pltpu.CompilerParams(vmem_limit_bytes=VMEM_LIMIT),
        cost_estimate=pl.CostEstimate(flops=flops, bytes_accessed=moved, transcendentals=0),
        name=name,
    )


def lane_of(shape):
    return lax.broadcasted_iota(jnp.int32, shape, 1)


def turn(values, amount):
    return pltpu.roll(values, amount % LANES, 1)


def tap_table(kernel, stack):
    count = kernel.shape[2]
    stack[...] = jnp.zeros_like(stack)
    for first in range(TAPS):
        stack[TAPS * first : TAPS * (first + 1), 0:count] = kernel[first]
    return stack[...].T[0:count].astype(BF16)


def weights_body(
    expand_one, reduce_one, pool, expand_two, reduce_two, kernel_one, kernel_two, *rest
):
    lines, (out, stack, turned_one, turned_two) = (rest[:-4], rest[-4:])
    hid_one, wide_one = (expand_one.shape[1], expand_one.shape[0])
    hid_two, wide_two = (expand_two.shape[1], expand_two.shape[0])
    out[0:hid_one, 0:wide_one] = expand_one[...].T
    out[hid_one : hid_one + wide_one, :] = reduce_one[...]
    base = hid_one + wide_one
    for quad in range(4):
        out[base : base + wide_one, 0:wide_one] = pool[quad].T
        base += wide_one
    out[base : base + kernel_two.shape[2], 0:LANES] = tap_table(kernel_two, turned_two)
    base += kernel_two.shape[2]
    out[base : base + hid_two, :] = expand_two[...].T
    base += hid_two
    for part in range(2):
        out[base : base + wide_two, :] = reduce_two[wide_two * part : wide_two * (part + 1), :].T
        base += wide_two
    stack[...] = jnp.zeros_like(stack)
    at = 0
    for line in lines:
        row = line[...].reshape(1, line.shape[0])
        for start in range(0, line.shape[0], wide_two):
            piece = row[:, start : start + wide_two]
            stack[at : at + 1, 0 : piece.shape[1]] = piece
            at += 1
    values = stack[...].T
    for part in range(3):
        rounded = values.astype(BF16)
        out[base : base + wide_two, LANES * part : LANES * part + LINES] = rounded
        values = values - rounded.astype(F32)
    base += wide_two
    out[base : base + kernel_one.shape[2], 0:LANES] = tap_table(kernel_one, turned_one)


def columns_of(ref):
    first, second, third = (
        ref[:, LANES * part : LANES * part + LINES].astype(F32) for part in range(3)
    )
    return first + (second + third)


def row_place(row, group):
    per = LANES // group // (2 * SIDE)
    return row // per, 2 * SIDE * (row % per)


def pack_rows(whole, sides, group):
    rows, channels = (whole.shape[0], whole.shape[1])
    width = LANES // group

    def step(index, carry):
        part = pl.ds(pl.multiple_of(index * 16, 16), 16)
        column = lane_of((16, LANES)) & (width - 1)
        inside = (column < SIDE) | (column >= width - SIDE)
        keep = jnp.where(inside, 1.0, 0.0).astype(BF16)
        sums = [None] * (2 * (sides.shape[1] // LANES))
        for row in range(rows):
            which, place = row_place(row, group)
            term = turn(whole[row, part, :] * keep, place + SIDE)
            at = 2 * which + row % 2
            sums[at] = term if sums[at] is None else sums[at] + term
        for which in range(sides.shape[1] // LANES):
            sides[part, LANES * which : LANES * (which + 1)] = sums[2 * which] + sums[2 * which + 1]
        return carry

    lax.fori_loop(0, channels // 16, step, 0)


def assemble_one_body(own, sib, outer, whole, sides):
    half = lax.axis_index("chan")
    count, group = (own.shape[0], own.shape[1])
    mine = pl.ds(pl.multiple_of(half * group, 16), group)
    other = pl.ds(pl.multiple_of((1 - half) * group, 16), group)
    rows = pl.ds(SIDE * (1 - half), count)
    edge = pl.ds(count * half, SIDE)
    whole[rows, mine, :] = own[...]
    whole[rows, other, :] = sib[...]
    whole[edge, other, :] = outer[:, 0:group, :]
    whole[edge, mine, :] = outer[:, group:, :]
    pack_rows(whole, sides, 1)


def assemble_two_body(pooled, from_sib, from_outer, whole, sides):
    top_is_outer = lax.axis_index("chan") == 0
    count, channels = (pooled.shape[0], pooled.shape[1])
    group = from_sib.shape[1]
    for row in range(count):
        whole[SIDE + row] = pooled[row]
    for start in range(0, channels, group):
        part = pl.ds(start, group)
        low = lane_of((group, LANES)) < LANES // 2
        sib = [from_sib[4 * k + start // group] for k in range(2)]
        out = [from_outer[4 * k + start // group] for k in range(2)]
        top0, top1 = (jnp.where(top_is_outer, out[k], sib[k]) for k in range(2))
        low0, low1 = (jnp.where(top_is_outer, sib[k], out[k]) for k in range(2))
        above = (top0, turn(top0, 64), top1)
        below = (turn(low0, 64), low0, turn(low1, 64))
        for k in range(SIDE):
            mid = turn(pooled[count - SIDE + k, part, :], 64)
            whole[k, part, :] = jnp.where(low, above[k], mid)
            mid = turn(pooled[k, part, :], 64)
            whole[SIDE + count + k, part, :] = jnp.where(low, mid, below[k])
    pack_rows(whole, sides, 2)


def tap_columns(tables, columns, which, taps, kbias, channels):
    half = lax.axis_index("chan")
    group = channels // 2
    for place, table, column in zip((half, 1 - half), tables, columns):
        part = pl.ds(pl.multiple_of(place * group, 16), group)
        values = table[:, 0:LANES].astype(F32)
        for tap in range(TAPS * TAPS):
            one = values[:, tap : tap + 1]
            taps[tap, part, :] = jnp.broadcast_to(one, (group, LANES)).astype(BF16)
        kbias[part, :] = jnp.broadcast_to(column[0:group, which : which + 1], (group, LANES))


def convolve(whole, left_in, right_in, taps, kbias, out, edges, group, high):
    rows, channels = (out.shape[0], out.shape[1])
    width = LANES // group

    def step(index, carry):
        part = pl.ds(pl.multiple_of(index * 16, 16), 16)
        lane = lane_of((16, LANES))
        column = (lane & (width - 1)).astype(jnp.int16)
        first = jnp.where(lax.rem(lane & (width - 1), 2 * SIDE) < SIDE, 1.0, 0.0).astype(BF16)
        merged = [
            left_in[part, LANES * k : LANES * (k + 1)] * first
            + right_in[part, LANES * k : LANES * (k + 1)] * (1 - first)
            for k in range(left_in.shape[1] // LANES)
        ]
        for k in range(rows + 2 * SIDE):
            which, at = row_place(k, group)
            edges[k] = turn(merged[which], width - SIDE - at)
        for start in range(0, rows, high):
            totals = [kbias[part, :] for _ in range(high)]
            for second in range(TAPS):
                shift = SIDE - second
                read = [whole[start + k, part, :] for k in range(high + TAPS - 1)]
                if shift != 0:
                    outside = (
                        column >= jnp.int16(width - shift)
                        if shift > 0
                        else column < jnp.int16(-shift)
                    )
                    read = [
                        turn(jnp.where(outside, edges[start + k], read[k]), shift)
                        for k in range(high + TAPS - 1)
                    ]
                weights = [taps[TAPS * first + second, part, :] for first in range(TAPS)]
                for k in range(high):
                    total = read[k] * weights[0]
                    for first in range(1, TAPS):
                        total = total + read[k + first] * weights[first]
                    totals[k] = totals[k] + total.astype(F32)
            for k in range(high):
                out[start + k, part, :] = totals[k].astype(BF16)
        return carry

    lax.fori_loop(0, channels // 16, step, 0, unroll=group)


def channel_norm(values, gain, shift):
    center = values - jnp.mean(values, axis=0, keepdims=True)
    spread = jnp.mean(center * center, axis=0, keepdims=True)
    return center * (lax.rsqrt(spread + 1e-06)) * gain + shift


def gelu(values):
    return 0.5 * values * (1.0 + lax.erf(values * 0.7071067811865476))


def dot(a, b):
    return jnp.dot(a, b, preferred_element_type=F32)


def fetch(packed, start, into, flags):
    rows = into.shape[1]
    return [
        pltpu.make_async_copy(ref.at[pl.ds(start, rows)], into.at[k], flags.at[k])
        for k, ref in enumerate(packed)
    ]


def section_one_body(
    whole, left_in, right_in, taps_own, taps_sib, columns_own, columns_sib, packed_own, packed_sib,
    out_own, to_sib, pooled, to_outer,
    taps, kbias, edges, conv, quads, ebias, reduce, weights, flags,
):
    half = lax.axis_index("chan")
    rows, channels = (conv.shape[0], conv.shape[1])
    group = channels // 2
    hidden = weights.shape[2]
    copies = fetch((packed_own, packed_sib), 0, weights, flags)
    for copy in copies:
        copy.start()
    columns = (columns_of(columns_own), columns_of(columns_sib))
    tap_columns((taps_own, taps_sib), columns, 0, taps, kbias, channels)
    for place in range(2):
        ebias[hidden * place : hidden * (place + 1), :] = columns[place][:, 1:2]
    convolve(whole, left_in, right_in, taps, kbias, conv, edges, 1, 16)
    for place, copy in enumerate(copies):
        copy.wait()
        at = hidden * place
        reduce[:, at : at + hidden] = weights[place, hidden : hidden + channels, :]
    named = columns[0][0:channels]
    taken = lax.broadcasted_iota(jnp.int32, (2 * LANES, 2 * LANES), 0)
    to = lax.broadcasted_iota(jnp.int32, (2 * LANES, 2 * LANES), 1)
    source = 2 * lax.rem(to, LANES) + lax.div(to, LANES)
    pick = jnp.where(taken == source, 1.0, 0.0).astype(BF16)
    first_rows = rows // 2

    def step(index, carry):
        order = [2 * index, 2 * index + first_rows, 2 * index + 1, 2 * index + 1 + first_rows]
        gain, shift, rbias, scale = (named[:, k : k + 1] for k in range(6, 10))
        pgain, pshift = (named[:, 10:11], named[:, 11:12])
        mixed = jnp.concatenate([conv[row].astype(F32) for row in order], axis=1)
        normed = channel_norm(mixed, gain, shift).astype(BF16)
        inner = [
            gelu(
                dot(weights[place, 0:hidden, 0:channels], normed)
                + ebias[hidden * place : hidden * (place + 1), :]
            ).astype(BF16)
            for place in range(2)
        ]
        summed = dot(reduce[...], jnp.concatenate(inner, axis=0))
        base = jnp.concatenate([whole[row + SIDE].astype(F32) for row in order], axis=1)
        block = (base + scale * (summed + rbias)).astype(BF16)
        for k, row in enumerate(order):
            low = block[0:group, LANES * k : LANES * (k + 1)]
            top = block[group:, LANES * k : LANES * (k + 1)]
            out_own[row] = jnp.where(half == 0, low, top)
            to_sib[row] = jnp.where(half == 0, top, low)
        pnorm = channel_norm(block.astype(F32), pgain, pshift).astype(BF16)
        for down in range(2):
            parted = dot(pnorm[:, 2 * LANES * down : 2 * LANES * (down + 1)], pick).astype(BF16)
            at = pl.ds(pl.multiple_of(index * LANES, LANES), LANES)
            quads[2 * down, :, at] = parted[:, 0:LANES]
            quads[2 * down + 1, :, at] = parted[:, LANES:]
        return carry

    lax.fori_loop(0, rows // 4, step, 0)
    base = hidden + channels
    for slot, place in enumerate((half, 1 - half)):
        total = None
        for quad in range(4):
            at = base + channels * quad
            term = dot(weights[slot, at : at + channels, 0:channels], quads[quad])
            total = term if total is None else total + term
        total = (total + columns[slot][0:channels, 2:3]).astype(BF16)
        part = pl.ds(pl.multiple_of(place * channels, 16), channels)
        for row in range(pooled.shape[0]):
            pooled[row, part, :] = total[:, LANES * row : LANES * (row + 1)]
    count = pooled.shape[0]
    for start in range(0, pooled.shape[1], group):
        part = pl.ds(start, group)
        low = lane_of((group, LANES)) < 64
        read = {k: pooled[k, part, :] for k in (0, 1, 2, count - 3, count - 2, count - 1)}
        top = (jnp.where(low, read[0], turn(read[1], 64)), read[2])
        bottom = (
            jnp.where(low, turn(read[count - 3], 64), read[count - 2]),
            turn(read[count - 1], 64),
        )
        for k in range(2):
            to_sib[rows + 4 * k + start // group] = jnp.where(half == 0, bottom[k], top[k])
            to_outer[4 * k + start // group] = jnp.where(half == 0, top[k], bottom[k])


def section_two_body(
    whole, left_in, right_in, taps_own, taps_sib, columns_own, columns_sib, packed_own, packed_sib,
    out_own, out_sib,
    taps, kbias, edges, conv, ebias, reduce, weights, flags,
):
    half = lax.axis_index("chan")
    rows, channels = (conv.shape[0], conv.shape[1])
    group = channels // 2
    hidden = 2 * channels
    copies = fetch((packed_own, packed_sib), weights.shape[1], weights, flags)
    for copy in copies:
        copy.start()
    columns = (columns_of(columns_own), columns_of(columns_sib))
    tap_columns((taps_own, taps_sib), columns, 3, taps, kbias, channels)
    for place in range(2):
        for part in range(2):
            at = hidden * place + channels * part
            ebias[at : at + channels, :] = columns[place][:, 4 + part : 5 + part]
    convolve(whole, left_in, right_in, taps, kbias, conv, edges, 2, rows)
    for place, copy in enumerate(copies):
        copy.wait()
        for part in range(2):
            at = hidden * place + channels * part
            rows_of = hidden + channels * part
            reduce[:, at : at + channels] = weights[place, rows_of : rows_of + channels, :]
    named = columns[0]

    def step(index, carry):
        order = [4 * index + k for k in range(4)]
        gain, shift, rbias, scale = (named[:, k : k + 1] for k in range(12, 16))
        mixed = jnp.concatenate([conv[row].astype(F32) for row in order], axis=1)
        normed = channel_norm(mixed, gain, shift).astype(BF16)
        inner = [
            gelu(
                dot(weights[place, 0:hidden, :], normed) + ebias[hidden * place : hidden * (place + 1), :]
            ).astype(BF16)
            for place in range(2)
        ]
        summed = dot(reduce[...], jnp.concatenate(inner, axis=0))
        base = jnp.concatenate([whole[row + SIDE].astype(F32) for row in order], axis=1)
        block = (base + scale * (summed + rbias)).astype(BF16)
        for k, row in enumerate(order):
            low = block[0:group, LANES * k : LANES * (k + 1)]
            top = block[group:, LANES * k : LANES * (k + 1)]
            out_own[row] = jnp.where(half == 0, low, top)
            out_sib[row] = jnp.where(half == 0, top, low)
        return carry

    lax.fori_loop(0, rows // 4, step, 0)


def on_device(
    image, kernel_one, kbias_one, gain_one, shift_one, expand_one, ebias_one, reduce_one,
    rbias_one, scale_one, pool_gain, pool_shift, pool_weight, pool_bias, kernel_two, kbias_two,
    gain_two, shift_two, expand_two, ebias_two, reduce_two, rbias_two, scale_two,
):
    half = lax.axis_index("chan")
    group, rows, cols = image.shape
    channels = 2 * group
    coarse_group = pool_weight.shape[2]
    coarse = 2 * coarse_group
    half_rows = rows // 2
    packed_rows = half_rows // 4
    n_row, n_col = (lax.axis_size("row"), lax.axis_size("col"))
    swap = [(0, 1), (1, 0)]
    outward = [(2 * r + 1, 2 * r + 2) for r in range(n_row - 1)]
    outward += [(b, a) for a, b in outward]
    right = [(c, c + 1) for c in range(n_col - 1)]
    left = [(b, a) for a, b in right]

    def to_sibling(x):
        return lax.ppermute(x, "chan", swap)

    def to_outer(x):
        return lax.ppermute(x, ("row", "chan"), outward)

    def in_order(mine, came):
        return jnp.where(half == 0, jnp.stack([mine, came]), jnp.stack([came, mine]))

    def sides(own_sides):
        return (lax.ppermute(own_sides, "col", right), lax.ppermute(own_sides, "col", left))

    turned = image.transpose(1, 0, 2)
    span = half_rows + SIDE
    own = lax.dynamic_slice_in_dim(turned, (half_rows - SIDE) * half, span, 0)
    sib = to_sibling(lax.dynamic_slice_in_dim(turned, (half_rows - SIDE) * (1 - half), span, 0))

    hid_one, hid_two = (expand_one.shape[1], expand_two.shape[1])
    first_rows = hid_one + 5 * channels
    total_rows = first_rows + coarse_group + 2 * hid_two + coarse + group
    own, reduce_one = lax.optimization_barrier((own, reduce_one))
    (packed_own,) = call(
        weights_body,
        [((total_rows, coarse), BF16)],
        [
            pltpu.VMEM((LINES, coarse), F32),
            pltpu.VMEM((LANES, LANES), F32),
            pltpu.VMEM((LANES, 2 * LANES), F32),
        ],
        moved=10**7,
        name="turn_weights",
    )(
        expand_one, reduce_one.T, pool_weight, expand_two, reduce_two,
        kernel_one.transpose(1, 2, 0), kernel_two.transpose(1, 2, 0),
        kbias_one, ebias_one, pool_bias, kbias_two, ebias_two, gain_one, shift_one, rbias_one,
        scale_one, pool_gain, pool_shift, gain_two, shift_two, rbias_two, scale_two,
    )
    packed_sib = to_sibling(packed_own)

    def block(rows, start):
        return pl.BlockSpec((rows, coarse), lambda _: (start // rows, 0))

    taps_two_spec = block(coarse_group, first_rows)
    columns_spec = block(coarse, total_rows - group - coarse)
    taps_one_spec = block(group, total_rows - group)
    full = pl.BlockSpec(memory_space=pltpu.VMEM)
    there = pl.BlockSpec(memory_space=pl.ANY)

    edge = [lax.dynamic_slice_in_dim(x, half_rows * half, SIDE, 0) for x in (own, sib)]
    outer = to_outer(jnp.concatenate(edge, axis=1))
    side_shape = ((channels, 2 * LANES), BF16)
    whole, own_sides = call(
        assemble_one_body,
        [((half_rows + 2 * SIDE, channels, LANES), BF16), side_shape],
        name="assemble_one",
    )(own, sib, outer)
    left_in, right_in = sides(own_sides)
    message_rows = 2 * coarse // group

    def scratch_for(wide, high, hid, fetched):
        return [
            pltpu.VMEM((TAPS * TAPS, wide, LANES), BF16),
            pltpu.VMEM((wide, LANES), F32),
            pltpu.VMEM((high + 2 * SIDE, 16, LANES), BF16),
            pltpu.VMEM((high, wide, LANES), BF16),
        ], [
            pltpu.VMEM((2 * hid, 1), F32),
            pltpu.VMEM((wide, 2 * hid), BF16),
            pltpu.VMEM((2, fetched, coarse), BF16),
            pltpu.SemaphoreType.DMA((2,)),
        ]

    before, after = scratch_for(channels, half_rows, hid_one, first_rows)
    block_own, for_sib, pooled, for_outer = call(
        section_one_body,
        [
            ((half_rows, group, LANES), BF16),
            ((half_rows + message_rows, group, LANES), BF16),
            ((packed_rows, coarse, LANES), BF16),
            ((message_rows, group, LANES), BF16),
        ],
        before + [pltpu.VMEM((4, channels, LANES * packed_rows), BF16)] + after,
        flops=10**10,
        moved=10**7,
        name="section_one",
        ins=[full] * 3 + [taps_one_spec] * 2 + [columns_spec] * 2 + [there] * 2,
    )(whole, left_in, right_in, *[packed_own, packed_sib] * 3)
    from_sib = to_sibling(for_sib)
    from_outer = to_outer(for_outer)
    block_came = from_sib[:half_rows]
    side_shape = ((coarse, 2 * LANES), BF16)
    whole_two, own_sides = call(
        assemble_two_body,
        [((packed_rows + 2 * SIDE, coarse, LANES), BF16), side_shape],
        name="assemble_two",
        ins=[full, pl.BlockSpec((message_rows, group, LANES), lambda _: (half_rows // message_rows, 0, 0)), full],
    )(pooled, from_sib, from_outer)
    left_in, right_in = sides(own_sides)
    block_one = in_order(block_own, block_came).reshape(rows, group, cols).transpose(1, 0, 2)
    whole_two, block_one = lax.optimization_barrier((whole_two, block_one))
    before, after = scratch_for(coarse, packed_rows, hid_two, 2 * hid_two)
    block_shape = ((packed_rows, coarse_group, LANES), BF16)
    two_block_own, two_block_sib = call(
        section_two_body,
        [block_shape, block_shape],
        before + after,
        flops=10**10,
        moved=10**7,
        name="section_two",
        ins=[full] * 3 + [taps_two_spec] * 2 + [columns_spec] * 2 + [there] * 2,
    )(whole_two, left_in, right_in, *[packed_own, packed_sib] * 3)
    two_came = to_sibling(two_block_sib)

    both = in_order(two_block_own, two_came)
    both = both.reshape(2, packed_rows, coarse_group, 2, cols // 2).transpose(2, 0, 3, 1, 4)
    block_two = both.reshape(coarse_group, half_rows, cols // 2)
    return (block_one, block_two)


def solution(mesh):
    tile = P("chan", "row", "col")
    return jax.shard_map(
        on_device,
        mesh=mesh,
        in_specs=(
            tile, P("chan", None, None), P("chan"), P(), P(), P(None, "chan"), P("chan"),
            P("chan", None), P(), P(), P(), P(), P(None, None, "chan"), P("chan"),
            P("chan", None, None), P("chan"), P(), P(), P(None, "chan"), P("chan"),
            P("chan", None), P(), P(),
        ),
        out_specs=(tile, tile),
        check_vma=False,
    )
```

```python
import functools

import jax
import jax.numpy as jnp
from jax import lax
from jax.experimental import pallas as pl
from jax.experimental.pallas import tpu as pltpu
from jax.sharding import PartitionSpec as P

F32 = jnp.float32
BF16 = jnp.bfloat16
LANES = 128
SIDE = 3
TAPS = 7
VMEM_LIMIT = 56 << 20
LINES = 16


def whole_block(shape):
    return pl.BlockSpec(shape, lambda _: (0,) * len(shape))


def call(body, outs, scratch=(), flops=0, moved=0, name=None, ins=None):
    def run(*operands):
        specs = [None] * len(operands) if ins is None else ins
        return pl.pallas_call(
            body,
            grid=(1,),
            in_specs=[
                whole_block(operand.shape) if spec is None else spec
                for operand, spec in zip(operands, specs)
            ],
            out_specs=tuple(whole_block(shape) for shape, _ in outs),
            out_shape=tuple(jax.ShapeDtypeStruct(shape, kind) for shape, kind in outs),
            scratch_shapes=list(scratch),
            compiler_params=pltpu.CompilerParams(vmem_limit_bytes=VMEM_LIMIT),
            cost_estimate=pl.CostEstimate(flops=flops, bytes_accessed=moved, transcendentals=0),
            name=name,
        )(*operands)

    return run


def lane_of(shape):
    return lax.broadcasted_iota(jnp.int32, shape, 1)


def turn(values, amount):
    return pltpu.roll(values, amount % LANES, 1)


def tap_table(kernel, stack):
    count = kernel.shape[2]
    stack[...] = jnp.zeros_like(stack)
    for first in range(TAPS):
        stack[TAPS * first : TAPS * (first + 1), 0:count] = kernel[first]
    return stack[...].T[0:count].astype(BF16)


def weights_body(
    expand_one, reduce_one, pool, expand_two, reduce_two, kernel_one, kernel_two, *rest
):
    lines, (out, stack, turned_one, turned_two) = (rest[:-4], rest[-4:])
    hid_one, wide_one = (expand_one.shape[1], expand_one.shape[0])
    hid_two, wide_two = (expand_two.shape[1], expand_two.shape[0])
    out[0:hid_one, 0:wide_one] = expand_one[...].T
    out[hid_one : hid_one + wide_one, :] = reduce_one[...]
    base = hid_one + wide_one
    for quad in range(4):
        out[base : base + wide_one, 0:wide_one] = pool[quad].T
        base += wide_one
    out[base : base + kernel_two.shape[2], 0:LANES] = tap_table(kernel_two, turned_two)
    base += kernel_two.shape[2]
    out[base : base + hid_two, :] = expand_two[...].T
    base += hid_two
    for part in range(2):
        out[base : base + wide_two, :] = reduce_two[wide_two * part : wide_two * (part + 1), :].T
        base += wide_two
    stack[...] = jnp.zeros_like(stack)
    at = 0
    for line in lines:
        row = line[...].reshape(1, line.shape[0])
        for start in range(0, line.shape[0], wide_two):
            piece = row[:, start : start + wide_two]
            stack[at : at + 1, 0 : piece.shape[1]] = piece
            at += 1
    values = stack[...].T
    for part in range(3):
        rounded = values.astype(BF16)
        out[base : base + wide_two, LANES * part : LANES * part + LINES] = rounded
        values = values - rounded.astype(F32)
    base += wide_two
    out[base : base + kernel_one.shape[2], 0:LANES] = tap_table(kernel_one, turned_one)


def columns_of(ref):
    first, second, third = (
        ref[:, LANES * part : LANES * part + LINES].astype(F32) for part in range(3)
    )
    return first + (second + third)


def row_place(row, group):
    per = LANES // group // (2 * SIDE)
    return row // per, 2 * SIDE * (row % per)


def pack_rows(whole, sides, group):
    rows, channels = (whole.shape[0], whole.shape[1])
    width = LANES // group

    def step(index, carry):
        part = pl.ds(pl.multiple_of(index * 16, 16), 16)
        column = lane_of((16, LANES)) & (width - 1)
        inside = (column < SIDE) | (column >= width - SIDE)
        keep = jnp.where(inside, 1.0, 0.0).astype(BF16)
        sums = [None] * (2 * (sides.shape[1] // LANES))
        for row in range(rows):
            which, place = row_place(row, group)
            term = turn(whole[row, part, :] * keep, place + SIDE)
            at = 2 * which + row % 2
            sums[at] = term if sums[at] is None else sums[at] + term
        for which in range(sides.shape[1] // LANES):
            sides[part, LANES * which : LANES * (which + 1)] = sums[2 * which] + sums[2 * which + 1]
        return carry

    lax.fori_loop(0, channels // 16, step, 0)


def assemble_one_body(own, sib, outer, whole, sides):
    half = lax.axis_index("chan")
    count, group = (own.shape[0], own.shape[1])
    mine = pl.ds(pl.multiple_of(half * group, 16), group)
    other = pl.ds(pl.multiple_of((1 - half) * group, 16), group)
    rows = pl.ds(SIDE * (1 - half), count)
    edge = pl.ds(count * half, SIDE)
    whole[rows, mine, :] = own[...]
    whole[rows, other, :] = sib[...]
    whole[edge, other, :] = outer[:, 0:group, :]
    whole[edge, mine, :] = outer[:, group:, :]
    pack_rows(whole, sides, 1)


def assemble_two_body(pooled, from_sib, from_outer, whole, sides):
    top_is_outer = lax.axis_index("chan") == 0
    count, channels = (pooled.shape[0], pooled.shape[1])
    group = from_sib.shape[1]
    for row in range(count):
        whole[SIDE + row] = pooled[row]
    for start in range(0, channels, group):
        part = pl.ds(start, group)
        low = lane_of((group, LANES)) < LANES // 2
        sib = [from_sib[4 * k + start // group] for k in range(2)]
        out = [from_outer[4 * k + start // group] for k in range(2)]
        top0, top1 = (jnp.where(top_is_outer, out[k], sib[k]) for k in range(2))
        low0, low1 = (jnp.where(top_is_outer, sib[k], out[k]) for k in range(2))
        above = (top0, turn(top0, 64), top1)
        below = (turn(low0, 64), low0, turn(low1, 64))
        for k in range(SIDE):
            mid = turn(pooled[count - SIDE + k, part, :], 64)
            whole[k, part, :] = jnp.where(low, above[k], mid)
            mid = turn(pooled[k, part, :], 64)
            whole[SIDE + count + k, part, :] = jnp.where(low, mid, below[k])
    pack_rows(whole, sides, 2)


def tap_columns(tables, columns, which, taps, kbias, channels):
    half = lax.axis_index("chan")
    group = channels // 2
    for place, table, column in zip((half, 1 - half), tables, columns):
        part = pl.ds(pl.multiple_of(place * group, 16), group)
        values = table[:, 0:LANES].astype(F32)
        for tap in range(TAPS * TAPS):
            one = values[:, tap : tap + 1]
            taps[tap, part, :] = jnp.broadcast_to(one, (group, LANES)).astype(BF16)
        kbias[part, :] = jnp.broadcast_to(column[0:group, which : which + 1], (group, LANES))


def convolve(whole, left_in, right_in, taps, kbias, out, edges, group, high):
    rows, channels = (out.shape[0], out.shape[1])
    width = LANES // group

    def step(index, carry):
        part = pl.ds(pl.multiple_of(index * 16, 16), 16)
        lane = lane_of((16, LANES))
        column = (lane & (width - 1)).astype(jnp.int16)
        first = jnp.where(lax.rem(lane & (width - 1), 2 * SIDE) < SIDE, 1.0, 0.0).astype(BF16)
        merged = [
            left_in[part, LANES * k : LANES * (k + 1)] * first
            + right_in[part, LANES * k : LANES * (k + 1)] * (1 - first)
            for k in range(left_in.shape[1] // LANES)
        ]
        for k in range(rows + 2 * SIDE):
            which, at = row_place(k, group)
            edges[k] = turn(merged[which], width - SIDE - at)
        for start in range(0, rows, high):
            totals = [kbias[part, :] for _ in range(high)]
            for second in range(TAPS):
                shift = SIDE - second
                read = [whole[start + k, part, :] for k in range(high + TAPS - 1)]
                if shift != 0:
                    outside = (
                        column >= jnp.int16(width - shift)
                        if shift > 0
                        else column < jnp.int16(-shift)
                    )
                    read = [
                        turn(jnp.where(outside, edges[start + k], read[k]), shift)
                        for k in range(high + TAPS - 1)
                    ]
                weights = [taps[TAPS * first + second, part, :] for first in range(TAPS)]
                for k in range(high):
                    total = read[k] * weights[0]
                    for first in range(1, TAPS):
                        total = total + read[k + first] * weights[first]
                    totals[k] = totals[k] + total.astype(F32)
            for k in range(high):
                out[start + k, part, :] = totals[k].astype(BF16)
        return carry

    lax.fori_loop(0, channels // 16, step, 0, unroll=group)


def channel_norm(values, gain, shift):
    center = values - jnp.mean(values, axis=0, keepdims=True)
    spread = jnp.mean(center * center, axis=0, keepdims=True)
    return center * (lax.rsqrt(spread + 1e-06)) * gain + shift


def gelu(values):
    return 0.5 * values * (1.0 + lax.erf(values * 0.7071067811865476))


def dot(a, b):
    return jnp.dot(a, b, preferred_element_type=F32)


def fetch(packed, start, into, flags):
    rows = into.shape[1]
    return [
        pltpu.make_async_copy(ref.at[pl.ds(start, rows)], into.at[k], flags.at[k])
        for k, ref in enumerate(packed)
    ]


def section_one_body(
    whole, left_in, right_in, taps_own, taps_sib, columns_own, columns_sib, packed_own, packed_sib,
    out_own, to_sib, pooled, to_outer,
    taps, kbias, edges, conv, quads, ebias, reduce, weights, flags,
):
    half = lax.axis_index("chan")
    rows, channels = (conv.shape[0], conv.shape[1])
    group = channels // 2
    hidden = weights.shape[2]
    copies = fetch((packed_own, packed_sib), 0, weights, flags)
    for copy in copies:
        copy.start()
    columns = (columns_of(columns_own), columns_of(columns_sib))
    tap_columns((taps_own, taps_sib), columns, 0, taps, kbias, channels)
    for place in range(2):
        ebias[hidden * place : hidden * (place + 1), :] = columns[place][:, 1:2]
    convolve(whole, left_in, right_in, taps, kbias, conv, edges, 1, 16)
    for place, copy in enumerate(copies):
        copy.wait()
        at = hidden * place
        reduce[:, at : at + hidden] = weights[place, hidden : hidden + channels, :]
    named = columns[0][0:channels]
    taken = lax.broadcasted_iota(jnp.int32, (2 * LANES, 2 * LANES), 0)
    to = lax.broadcasted_iota(jnp.int32, (2 * LANES, 2 * LANES), 1)
    source = 2 * lax.rem(to, LANES) + lax.div(to, LANES)
    pick = jnp.where(taken == source, 1.0, 0.0).astype(BF16)
    first_rows = rows // 2

    def step(index, carry):
        order = [2 * index, 2 * index + first_rows, 2 * index + 1, 2 * index + 1 + first_rows]
        gain, shift, rbias, scale = (named[:, k : k + 1] for k in range(6, 10))
        pgain, pshift = (named[:, 10:11], named[:, 11:12])
        mixed = jnp.concatenate([conv[row].astype(F32) for row in order], axis=1)
        normed = channel_norm(mixed, gain, shift).astype(BF16)
        inner = [
            gelu(
                dot(weights[place, 0:hidden, 0:channels], normed)
                + ebias[hidden * place : hidden * (place + 1), :]
            ).astype(BF16)
            for place in range(2)
        ]
        summed = dot(reduce[...], jnp.concatenate(inner, axis=0))
        base = jnp.concatenate([whole[row + SIDE].astype(F32) for row in order], axis=1)
        block = (base + scale * (summed + rbias)).astype(BF16)
        for k, row in enumerate(order):
            low = block[0:group, LANES * k : LANES * (k + 1)]
            top = block[group:, LANES * k : LANES * (k + 1)]
            out_own[row] = jnp.where(half == 0, low, top)
            to_sib[row] = jnp.where(half == 0, top, low)
        pnorm = channel_norm(block.astype(F32), pgain, pshift).astype(BF16)
        for down in range(2):
            parted = dot(pnorm[:, 2 * LANES * down : 2 * LANES * (down + 1)], pick).astype(BF16)
            at = pl.ds(pl.multiple_of(index * LANES, LANES), LANES)
            quads[2 * down, :, at] = parted[:, 0:LANES]
            quads[2 * down + 1, :, at] = parted[:, LANES:]
        return carry

    lax.fori_loop(0, rows // 4, step, 0, unroll=2)
    base = hidden + channels
    for slot, place in enumerate((half, 1 - half)):
        total = None
        for quad in range(4):
            at = base + channels * quad
            term = dot(weights[slot, at : at + channels, 0:channels], quads[quad])
            total = term if total is None else total + term
        total = (total + columns[slot][0:channels, 2:3]).astype(BF16)
        part = pl.ds(pl.multiple_of(place * channels, 16), channels)
        for row in range(pooled.shape[0]):
            pooled[row, part, :] = total[:, LANES * row : LANES * (row + 1)]
    count = pooled.shape[0]
    for start in range(0, pooled.shape[1], group):
        part = pl.ds(start, group)
        low = lane_of((group, LANES)) < 64
        read = {k: pooled[k, part, :] for k in (0, 1, 2, count - 3, count - 2, count - 1)}
        top = (jnp.where(low, read[0], turn(read[1], 64)), read[2])
        bottom = (
            jnp.where(low, turn(read[count - 3], 64), read[count - 2]),
            turn(read[count - 1], 64),
        )
        for k in range(2):
            to_sib[rows + 4 * k + start // group] = jnp.where(half == 0, bottom[k], top[k])
            to_outer[4 * k + start // group] = jnp.where(half == 0, top[k], bottom[k])


def section_two_body(
    whole, left_in, right_in, taps_own, taps_sib, columns_own, columns_sib, packed_own, packed_sib,
    out_own, out_sib,
    taps, kbias, edges, conv, ebias, reduce, weights, flags,
):
    half = lax.axis_index("chan")
    rows, channels = (conv.shape[0], conv.shape[1])
    group = channels // 2
    hidden = 2 * channels
    copies = fetch((packed_own, packed_sib), weights.shape[1], weights, flags)
    for copy in copies:
        copy.start()
    columns = (columns_of(columns_own), columns_of(columns_sib))
    tap_columns((taps_own, taps_sib), columns, 3, taps, kbias, channels)
    for place in range(2):
        for part in range(2):
            at = hidden * place + channels * part
            ebias[at : at + channels, :] = columns[place][:, 4 + part : 5 + part]
    convolve(whole, left_in, right_in, taps, kbias, conv, edges, 2, rows)
    for place, copy in enumerate(copies):
        copy.wait()
        for part in range(2):
            at = hidden * place + channels * part
            rows_of = hidden + channels * part
            reduce[:, at : at + channels] = weights[place, rows_of : rows_of + channels, :]
    named = columns[0]

    def step(index, carry):
        order = [4 * index + k for k in range(4)]
        gain, shift, rbias, scale = (named[:, k : k + 1] for k in range(12, 16))
        mixed = jnp.concatenate([conv[row].astype(F32) for row in order], axis=1)
        normed = channel_norm(mixed, gain, shift).astype(BF16)
        inner = [
            gelu(
                dot(weights[place, 0:hidden, :], normed) + ebias[hidden * place : hidden * (place + 1), :]
            ).astype(BF16)
            for place in range(2)
        ]
        summed = dot(reduce[...], jnp.concatenate(inner, axis=0))
        base = jnp.concatenate([whole[row + SIDE].astype(F32) for row in order], axis=1)
        block = (base + scale * (summed + rbias)).astype(BF16)
        for k, row in enumerate(order):
            low = block[0:group, LANES * k : LANES * (k + 1)]
            top = block[group:, LANES * k : LANES * (k + 1)]
            out_own[row] = jnp.where(half == 0, low, top)
            out_sib[row] = jnp.where(half == 0, top, low)
        return carry

    lax.fori_loop(0, rows // 4, step, 0, unroll=2)


def on_device(
    image, kernel_one, kbias_one, gain_one, shift_one, expand_one, ebias_one, reduce_one,
    rbias_one, scale_one, pool_gain, pool_shift, pool_weight, pool_bias, kernel_two, kbias_two,
    gain_two, shift_two, expand_two, ebias_two, reduce_two, rbias_two, scale_two,
):
    half = lax.axis_index("chan")
    group, rows, cols = image.shape
    channels = 2 * group
    coarse_group = pool_weight.shape[2]
    coarse = 2 * coarse_group
    half_rows = rows // 2
    packed_rows = half_rows // 4
    n_row, n_col = (lax.axis_size("row"), lax.axis_size("col"))
    swap = [(0, 1), (1, 0)]
    outward = [(2 * r + 1, 2 * r + 2) for r in range(n_row - 1)]
    outward += [(b, a) for a, b in outward]
    right = [(c, c + 1) for c in range(n_col - 1)]
    left = [(b, a) for a, b in right]

    def to_sibling(x):
        return lax.ppermute(x, "chan", swap)

    def to_outer(x):
        return lax.ppermute(x, ("row", "chan"), outward)

    def in_order(mine, came):
        return jnp.where(half == 0, jnp.stack([mine, came]), jnp.stack([came, mine]))

    def sides(own_sides):
        return (lax.ppermute(own_sides, "col", right), lax.ppermute(own_sides, "col", left))

    turned = image.transpose(1, 0, 2)
    span = half_rows + SIDE
    own = lax.dynamic_slice_in_dim(turned, (half_rows - SIDE) * half, span, 0)
    sib = to_sibling(lax.dynamic_slice_in_dim(turned, (half_rows - SIDE) * (1 - half), span, 0))

    hid_one, hid_two = (expand_one.shape[1], expand_two.shape[1])
    first_rows = hid_one + 5 * channels
    total_rows = first_rows + coarse_group + 2 * hid_two + coarse + group
    (packed_own,) = call(
        weights_body,
        [((total_rows, coarse), BF16)],
        [
            pltpu.VMEM((LINES, coarse), F32),
            pltpu.VMEM((LANES, LANES), F32),
            pltpu.VMEM((LANES, 2 * LANES), F32),
        ],
        moved=10**7,
        name="turn_weights",
    )(
        expand_one, reduce_one.T, pool_weight, expand_two, reduce_two,
        kernel_one.transpose(1, 2, 0), kernel_two.transpose(1, 2, 0),
        kbias_one, ebias_one, pool_bias, kbias_two, ebias_two, gain_one, shift_one, rbias_one,
        scale_one, pool_gain, pool_shift, gain_two, shift_two, rbias_two, scale_two,
    )
    packed_own, sib = lax.optimization_barrier((packed_own, sib))
    packed_sib = to_sibling(packed_own)

    def block(rows, start):
        return pl.BlockSpec((rows, coarse), lambda _: (start // rows, 0))

    taps_two_spec = block(coarse_group, first_rows)
    columns_spec = block(coarse, total_rows - group - coarse)
    taps_one_spec = block(group, total_rows - group)
    there = pl.BlockSpec(memory_space=pl.ANY)

    edge = [lax.dynamic_slice_in_dim(x, half_rows * half, SIDE, 0) for x in (own, sib)]
    outer = to_outer(jnp.concatenate(edge, axis=1))
    side_shape = ((channels, 2 * LANES), BF16)
    whole, own_sides = call(
        assemble_one_body,
        [((half_rows + 2 * SIDE, channels, LANES), BF16), side_shape],
        name="assemble_one",
    )(own, sib, outer)
    left_in, right_in = sides(own_sides)
    message_rows = 2 * coarse // group

    def scratch_for(wide, high, hid, fetched):
        return [
            pltpu.VMEM((TAPS * TAPS, wide, LANES), BF16),
            pltpu.VMEM((wide, LANES), F32),
            pltpu.VMEM((high + 2 * SIDE, 16, LANES), BF16),
            pltpu.VMEM((high, wide, LANES), BF16),
        ], [
            pltpu.VMEM((2 * hid, 1), F32),
            pltpu.VMEM((wide, 2 * hid), BF16),
            pltpu.VMEM((2, fetched, coarse), BF16),
            pltpu.SemaphoreType.DMA((2,)),
        ]

    before, after = scratch_for(channels, half_rows, hid_one, first_rows)
    block_own, for_sib, pooled, for_outer = call(
        section_one_body,
        [
            ((half_rows, group, LANES), BF16),
            ((half_rows + message_rows, group, LANES), BF16),
            ((packed_rows, coarse, LANES), BF16),
            ((message_rows, group, LANES), BF16),
        ],
        before + [pltpu.VMEM((4, channels, LANES * packed_rows), BF16)] + after,
        flops=10**10,
        moved=10**7,
        name="section_one",
        ins=[None] * 3 + [taps_one_spec] * 2 + [columns_spec] * 2 + [there] * 2,
    )(whole, left_in, right_in, *[packed_own, packed_sib] * 3)
    from_sib = to_sibling(for_sib)
    from_outer = to_outer(for_outer)
    block_came = from_sib[:half_rows]
    side_shape = ((coarse, 2 * LANES), BF16)
    whole_two, own_sides = call(
        assemble_two_body,
        [((packed_rows + 2 * SIDE, coarse, LANES), BF16), side_shape],
        name="assemble_two",
        ins=[
            None,
            pl.BlockSpec((message_rows, group, LANES), lambda _: (half_rows // message_rows, 0, 0)),
            None,
        ],
    )(pooled, from_sib, from_outer)
    left_in, right_in = sides(own_sides)
    block_one = in_order(block_own, block_came).reshape(rows, group, cols).transpose(1, 0, 2)
    whole_two, block_one = lax.optimization_barrier((whole_two, block_one))
    before, after = scratch_for(coarse, packed_rows, hid_two, 2 * hid_two)
    block_shape = ((packed_rows, coarse_group, LANES), BF16)
    two_block_own, two_block_sib = call(
        section_two_body,
        [block_shape, block_shape],
        before + after,
        flops=10**10,
        moved=10**7,
        name="section_two",
        ins=[None] * 3 + [taps_two_spec] * 2 + [columns_spec] * 2 + [there] * 2,
    )(whole_two, left_in, right_in, *[packed_own, packed_sib] * 3)
    two_came = to_sibling(two_block_sib)

    both = in_order(two_block_own, two_came)
    both = both.reshape(2, packed_rows, coarse_group, 2, cols // 2).transpose(2, 0, 3, 1, 4)
    block_two = both.reshape(coarse_group, half_rows, cols // 2)
    return (block_one, block_two)


def solution(mesh):
    tile = P("chan", "row", "col")
    return jax.shard_map(
        on_device,
        mesh=mesh,
        in_specs=(
            tile, P("chan", None, None), P("chan"), P(), P(), P(None, "chan"), P("chan"),
            P("chan", None), P(), P(), P(), P(), P(None, None, "chan"), P("chan"),
            P("chan", None, None), P("chan"), P(), P(), P(None, "chan"), P("chan"),
            P("chan", None), P(), P(),
        ),
        out_specs=(tile, tile),
        check_vma=False,
    )
```

```python
import functools

import jax
import jax.numpy as jnp
from jax import lax
from jax.experimental import pallas as pl
from jax.experimental.pallas import tpu as pltpu
from jax.sharding import PartitionSpec as P

F32 = jnp.float32
BF16 = jnp.bfloat16
LANES = 128
SIDE = 3
TAPS = 7
VMEM_LIMIT = 56 << 20
LINES = 16


def whole_block(shape):
    return pl.BlockSpec(shape, lambda _: (0,) * len(shape))


def call(body, outs, scratch=(), flops=0, moved=0, name=None, ins=None):
    def run(*operands):
        specs = [None] * len(operands) if ins is None else ins
        return pl.pallas_call(
            body,
            grid=(1,),
            in_specs=[
                whole_block(operand.shape) if spec is None else spec
                for operand, spec in zip(operands, specs)
            ],
            out_specs=tuple(whole_block(shape) for shape, _ in outs),
            out_shape=tuple(jax.ShapeDtypeStruct(shape, kind) for shape, kind in outs),
            scratch_shapes=list(scratch),
            compiler_params=pltpu.CompilerParams(vmem_limit_bytes=VMEM_LIMIT),
            cost_estimate=pl.CostEstimate(flops=flops, bytes_accessed=moved, transcendentals=0),
            name=name,
        )(*operands)

    return run


def lane_of(shape):
    return lax.broadcasted_iota(jnp.int32, shape, 1)


def turn(values, amount):
    return pltpu.roll(values, amount % LANES, 1)


def tap_table(kernel, stack):
    count = kernel.shape[2]
    stack[...] = jnp.zeros_like(stack)
    for first in range(TAPS):
        stack[TAPS * first : TAPS * (first + 1), 0:count] = kernel[first]
    return stack[...].T[0:count].astype(BF16)


def weights_body(
    expand_one, reduce_one, pool, expand_two, reduce_two, kernel_one, kernel_two, *rest
):
    lines, (out, stack, turned_one, turned_two) = (rest[:-4], rest[-4:])
    hid_one, wide_one = (expand_one.shape[1], expand_one.shape[0])
    hid_two, wide_two = (expand_two.shape[1], expand_two.shape[0])
    out[0:hid_one, 0:wide_one] = expand_one[...].T
    out[hid_one : hid_one + wide_one, :] = reduce_one[...]
    base = hid_one + wide_one
    for quad in range(4):
        out[base : base + wide_one, 0:wide_one] = pool[quad].T
        base += wide_one
    out[base : base + kernel_two.shape[2], 0:LANES] = tap_table(kernel_two, turned_two)
    base += kernel_two.shape[2]
    out[base : base + hid_two, :] = expand_two[...].T
    base += hid_two
    for part in range(2):
        out[base : base + wide_two, :] = reduce_two[wide_two * part : wide_two * (part + 1), :].T
        base += wide_two
    stack[...] = jnp.zeros_like(stack)
    at = 0
    for line in lines:
        row = line[...].reshape(1, line.shape[0])
        for start in range(0, line.shape[0], wide_two):
            piece = row[:, start : start + wide_two]
            stack[at : at + 1, 0 : piece.shape[1]] = piece
            at += 1
    values = stack[...].T
    for part in range(3):
        rounded = values.astype(BF16)
        out[base : base + wide_two, LANES * part : LANES * part + LINES] = rounded
        values = values - rounded.astype(F32)
    base += wide_two
    out[base : base + kernel_one.shape[2], 0:LANES] = tap_table(kernel_one, turned_one)


def columns_of(ref):
    first, second, third = (
        ref[:, LANES * part : LANES * part + LINES].astype(F32) for part in range(3)
    )
    return first + (second + third)


def row_place(row, group):
    per = LANES // group // (2 * SIDE)
    return row // per, 2 * SIDE * (row % per)


def pack_rows(whole, sides, group):
    rows, channels = (whole.shape[0], whole.shape[1])
    width = LANES // group

    def step(index, carry):
        part = pl.ds(pl.multiple_of(index * 16, 16), 16)
        column = lane_of((16, LANES)) & (width - 1)
        inside = (column < SIDE) | (column >= width - SIDE)
        keep = jnp.where(inside, 1.0, 0.0).astype(BF16)
        sums = [None] * (2 * (sides.shape[1] // LANES))
        for row in range(rows):
            which, place = row_place(row, group)
            term = turn(whole[row, part, :] * keep, place + SIDE)
            at = 2 * which + row % 2
            sums[at] = term if sums[at] is None else sums[at] + term
        for which in range(sides.shape[1] // LANES):
            sides[part, LANES * which : LANES * (which + 1)] = sums[2 * which] + sums[2 * which + 1]
        return carry

    lax.fori_loop(0, channels // 16, step, 0)


def assemble_one_body(own, sib, outer, whole, sides):
    half = lax.axis_index("chan")
    count, group = (own.shape[0], own.shape[1])
    mine = pl.ds(pl.multiple_of(half * group, 16), group)
    other = pl.ds(pl.multiple_of((1 - half) * group, 16), group)
    rows = pl.ds(SIDE * (1 - half), count)
    edge = pl.ds(count * half, SIDE)
    whole[rows, mine, :] = own[...]
    whole[rows, other, :] = sib[...]
    whole[edge, other, :] = outer[:, 0:group, :]
    whole[edge, mine, :] = outer[:, group:, :]
    pack_rows(whole, sides, 1)


def assemble_two_body(pooled, from_sib, from_outer, whole, sides):
    top_is_outer = lax.axis_index("chan") == 0
    count, channels = (pooled.shape[0], pooled.shape[1])
    group = from_sib.shape[1]
    for row in range(count):
        whole[SIDE + row] = pooled[row]
    for start in range(0, channels, group):
        part = pl.ds(start, group)
        low = lane_of((group, LANES)) < LANES // 2
        sib = [from_sib[4 * k + start // group] for k in range(2)]
        out = [from_outer[4 * k + start // group] for k in range(2)]
        top0, top1 = (jnp.where(top_is_outer, out[k], sib[k]) for k in range(2))
        low0, low1 = (jnp.where(top_is_outer, sib[k], out[k]) for k in range(2))
        above = (top0, turn(top0, 64), top1)
        below = (turn(low0, 64), low0, turn(low1, 64))
        for k in range(SIDE):
            mid = turn(pooled[count - SIDE + k, part, :], 64)
            whole[k, part, :] = jnp.where(low, above[k], mid)
            mid = turn(pooled[k, part, :], 64)
            whole[SIDE + count + k, part, :] = jnp.where(low, mid, below[k])
    pack_rows(whole, sides, 2)


def tap_columns(tables, columns, which, taps, kbias, channels):
    half = lax.axis_index("chan")
    group = channels // 2
    for place, table, column in zip((half, 1 - half), tables, columns):
        part = pl.ds(pl.multiple_of(place * group, 16), group)
        values = table[:, 0:LANES].astype(F32)
        for tap in range(TAPS * TAPS):
            one = values[:, tap : tap + 1]
            taps[tap, part, :] = jnp.broadcast_to(one, (group, LANES)).astype(BF16)
        kbias[part, :] = jnp.broadcast_to(column[0:group, which : which + 1], (group, LANES))


def convolve(whole, left_in, right_in, taps, kbias, out, edges, group, high):
    rows, channels = (out.shape[0], out.shape[1])
    width = LANES // group

    def step(index, carry):
        part = pl.ds(pl.multiple_of(index * 16, 16), 16)
        lane = lane_of((16, LANES))
        column = (lane & (width - 1)).astype(jnp.int16)
        first = jnp.where(lax.rem(lane & (width - 1), 2 * SIDE) < SIDE, 1.0, 0.0).astype(BF16)
        merged = [
            left_in[part, LANES * k : LANES * (k + 1)] * first
            + right_in[part, LANES * k : LANES * (k + 1)] * (1 - first)
            for k in range(left_in.shape[1] // LANES)
        ]
        for k in range(rows + 2 * SIDE):
            which, at = row_place(k, group)
            edges[k] = turn(merged[which], width - SIDE - at)
        for start in range(0, rows, high):
            totals = [kbias[part, :] for _ in range(high)]
            for second in range(TAPS):
                shift = SIDE - second
                read = [whole[start + k, part, :] for k in range(high + TAPS - 1)]
                if shift != 0:
                    outside = (
                        column >= jnp.int16(width - shift)
                        if shift > 0
                        else column < jnp.int16(-shift)
                    )
                    read = [
                        turn(jnp.where(outside, edges[start + k], read[k]), shift)
                        for k in range(high + TAPS - 1)
                    ]
                weights = [taps[TAPS * first + second, part, :] for first in range(TAPS)]
                for k in range(high):
                    total = read[k] * weights[0]
                    for first in range(1, TAPS):
                        total = total + read[k + first] * weights[first]
                    totals[k] = totals[k] + total.astype(F32)
            for k in range(high):
                out[start + k, part, :] = totals[k].astype(BF16)
        return carry

    lax.fori_loop(0, channels // 16, step, 0, unroll=group)


def channel_norm(values, gain, shift):
    center = values - jnp.mean(values, axis=0, keepdims=True)
    spread = jnp.mean(center * center, axis=0, keepdims=True)
    return center * (lax.rsqrt(spread + 1e-06)) * gain + shift


def gelu(values):
    return 0.5 * values * (1.0 + lax.erf(values * 0.7071067811865476))


def dot(a, b):
    return jnp.dot(a, b, preferred_element_type=F32)


def fetch(packed, start, into, flags):
    rows = into.shape[1]
    return [
        pltpu.make_async_copy(ref.at[pl.ds(start, rows)], into.at[k], flags.at[k])
        for k, ref in enumerate(packed)
    ]


def section_one_body(
    whole, left_in, right_in, taps_own, taps_sib, columns_own, columns_sib, packed_own, packed_sib,
    out_own, to_sib, pooled, to_outer,
    taps, kbias, edges, conv, quads, ebias, reduce, weights, flags,
):
    half = lax.axis_index("chan")
    rows, channels = (conv.shape[0], conv.shape[1])
    group = channels // 2
    hidden = weights.shape[2]
    copies = fetch((packed_own, packed_sib), 0, weights, flags)
    for copy in copies:
        copy.start()
    columns = (columns_of(columns_own), columns_of(columns_sib))
    tap_columns((taps_own, taps_sib), columns, 0, taps, kbias, channels)
    for place in range(2):
        ebias[hidden * place : hidden * (place + 1), :] = columns[place][:, 1:2]
    convolve(whole, left_in, right_in, taps, kbias, conv, edges, 1, 16)
    for place, copy in enumerate(copies):
        copy.wait()
        at = hidden * place
        reduce[:, at : at + hidden] = weights[place, hidden : hidden + channels, :]
    named = columns[0][0:channels]
    taken = lax.broadcasted_iota(jnp.int32, (2 * LANES, 2 * LANES), 0)
    to = lax.broadcasted_iota(jnp.int32, (2 * LANES, 2 * LANES), 1)
    source = 2 * lax.rem(to, LANES) + lax.div(to, LANES)
    pick = jnp.where(taken == source, 1.0, 0.0).astype(BF16)
    first_rows = rows // 2

    def step(index, carry):
        order = [2 * index, 2 * index + first_rows, 2 * index + 1, 2 * index + 1 + first_rows]
        gain, shift, rbias, scale = (named[:, k : k + 1] for k in range(6, 10))
        pgain, pshift = (named[:, 10:11], named[:, 11:12])
        mixed = jnp.concatenate([conv[row].astype(F32) for row in order], axis=1)
        normed = channel_norm(mixed, gain, shift).astype(BF16)
        inner = [
            gelu(
                dot(weights[place, 0:hidden, 0:channels], normed)
                + ebias[hidden * place : hidden * (place + 1), :]
            ).astype(BF16)
            for place in range(2)
        ]
        summed = dot(reduce[...], jnp.concatenate(inner, axis=0))
        base = jnp.concatenate([whole[row + SIDE].astype(F32) for row in order], axis=1)
        block = (base + scale * (summed + rbias)).astype(BF16)
        for k, row in enumerate(order):
            low = block[0:group, LANES * k : LANES * (k + 1)]
            top = block[group:, LANES * k : LANES * (k + 1)]
            out_own[row] = jnp.where(half == 0, low, top)
            to_sib[row] = jnp.where(half == 0, top, low)
        pnorm = channel_norm(block.astype(F32), pgain, pshift).astype(BF16)
        for down in range(2):
            parted = dot(pnorm[:, 2 * LANES * down : 2 * LANES * (down + 1)], pick).astype(BF16)
            at = pl.ds(pl.multiple_of(index * LANES, LANES), LANES)
            quads[2 * down, :, at] = parted[:, 0:LANES]
            quads[2 * down + 1, :, at] = parted[:, LANES:]
        return carry

    lax.fori_loop(0, rows // 4, step, 0, unroll=2)
    base = hidden + channels
    for slot, place in enumerate((half, 1 - half)):
        total = None
        for quad in range(4):
            at = base + channels * quad
            term = dot(weights[slot, at : at + channels, 0:channels], quads[quad])
            total = term if total is None else total + term
        total = (total + columns[slot][0:channels, 2:3]).astype(BF16)
        part = pl.ds(pl.multiple_of(place * channels, 16), channels)
        for row in range(pooled.shape[0]):
            pooled[row, part, :] = total[:, LANES * row : LANES * (row + 1)]
    count = pooled.shape[0]
    for start in range(0, pooled.shape[1], group):
        part = pl.ds(start, group)
        low = lane_of((group, LANES)) < 64
        read = {k: pooled[k, part, :] for k in (0, 1, 2, count - 3, count - 2, count - 1)}
        top = (jnp.where(low, read[0], turn(read[1], 64)), read[2])
        bottom = (
            jnp.where(low, turn(read[count - 3], 64), read[count - 2]),
            turn(read[count - 1], 64),
        )
        for k in range(2):
            to_sib[rows + 4 * k + start // group] = jnp.where(half == 0, bottom[k], top[k])
            to_outer[4 * k + start // group] = jnp.where(half == 0, top[k], bottom[k])


def section_two_body(
    whole, left_in, right_in, taps_own, taps_sib, columns_own, columns_sib, packed_own, packed_sib,
    out_own, out_sib,
    taps, kbias, edges, conv, ebias, reduce, weights, flags,
):
    half = lax.axis_index("chan")
    rows, channels = (conv.shape[0], conv.shape[1])
    group = channels // 2
    hidden = 2 * channels
    copies = fetch((packed_own, packed_sib), weights.shape[1], weights, flags)
    for copy in copies:
        copy.start()
    columns = (columns_of(columns_own), columns_of(columns_sib))
    tap_columns((taps_own, taps_sib), columns, 3, taps, kbias, channels)
    for place in range(2):
        for part in range(2):
            at = hidden * place + channels * part
            ebias[at : at + channels, :] = columns[place][:, 4 + part : 5 + part]
    convolve(whole, left_in, right_in, taps, kbias, conv, edges, 2, rows)
    for place, copy in enumerate(copies):
        copy.wait()
        for part in range(2):
            at = hidden * place + channels * part
            rows_of = hidden + channels * part
            reduce[:, at : at + channels] = weights[place, rows_of : rows_of + channels, :]
    named = columns[0]

    def step(index, carry):
        order = [4 * index + k for k in range(4)]
        gain, shift, rbias, scale = (named[:, k : k + 1] for k in range(12, 16))
        mixed = jnp.concatenate([conv[row].astype(F32) for row in order], axis=1)
        normed = channel_norm(mixed, gain, shift).astype(BF16)
        inner = [
            gelu(
                dot(weights[place, 0:hidden, :], normed) + ebias[hidden * place : hidden * (place + 1), :]
            ).astype(BF16)
            for place in range(2)
        ]
        summed = dot(reduce[...], jnp.concatenate(inner, axis=0))
        base = jnp.concatenate([whole[row + SIDE].astype(F32) for row in order], axis=1)
        block = (base + scale * (summed + rbias)).astype(BF16)
        for k, row in enumerate(order):
            low = block[0:group, LANES * k : LANES * (k + 1)]
            top = block[group:, LANES * k : LANES * (k + 1)]
            out_own[row] = jnp.where(half == 0, low, top)
            out_sib[row] = jnp.where(half == 0, top, low)
        return carry

    lax.fori_loop(0, rows // 4, step, 0, unroll=2)


def on_device(
    image, kernel_one, kbias_one, gain_one, shift_one, expand_one, ebias_one, reduce_one,
    rbias_one, scale_one, pool_gain, pool_shift, pool_weight, pool_bias, kernel_two, kbias_two,
    gain_two, shift_two, expand_two, ebias_two, reduce_two, rbias_two, scale_two,
):
    half = lax.axis_index("chan")
    group, rows, cols = image.shape
    channels = 2 * group
    coarse_group = pool_weight.shape[2]
    coarse = 2 * coarse_group
    half_rows = rows // 2
    packed_rows = half_rows // 4
    n_row, n_col = (lax.axis_size("row"), lax.axis_size("col"))
    swap = [(0, 1), (1, 0)]
    outward = [(2 * r + 1, 2 * r + 2) for r in range(n_row - 1)]
    outward += [(b, a) for a, b in outward]
    right = [(c, c + 1) for c in range(n_col - 1)]
    left = [(b, a) for a, b in right]

    def to_sibling(x):
        return lax.ppermute(x, "chan", swap)

    def to_outer(x):
        return lax.ppermute(x, ("row", "chan"), outward)

    def in_order(mine, came):
        return jnp.where(half == 0, jnp.stack([mine, came]), jnp.stack([came, mine]))

    def sides(own_sides):
        return (lax.ppermute(own_sides, "col", right), lax.ppermute(own_sides, "col", left))

    turned = image.transpose(1, 0, 2)
    span = half_rows + SIDE
    sib = to_sibling(lax.dynamic_slice_in_dim(turned, (half_rows - SIDE) * (1 - half), span, 0))

    hid_one, hid_two = (expand_one.shape[1], expand_two.shape[1])
    first_rows = hid_one + 5 * channels
    total_rows = first_rows + coarse_group + 2 * hid_two + coarse + group
    (packed_own,) = call(
        weights_body,
        [((total_rows, coarse), BF16)],
        [
            pltpu.VMEM((LINES, coarse), F32),
            pltpu.VMEM((LANES, LANES), F32),
            pltpu.VMEM((LANES, 2 * LANES), F32),
        ],
        moved=10**7,
        name="turn_weights",
    )(
        expand_one, reduce_one.T, pool_weight, expand_two, reduce_two,
        kernel_one.transpose(1, 2, 0), kernel_two.transpose(1, 2, 0),
        kbias_one, ebias_one, pool_bias, kbias_two, ebias_two, gain_one, shift_one, rbias_one,
        scale_one, pool_gain, pool_shift, gain_two, shift_two, rbias_two, scale_two,
    )
    packed_own, sib, image = lax.optimization_barrier((packed_own, sib, image))
    own_at = (half_rows - SIDE) * half
    own = lax.dynamic_slice_in_dim(image, own_at, span, 1).transpose(1, 0, 2)
    packed_sib = to_sibling(packed_own)

    def block(rows, start):
        return pl.BlockSpec((rows, coarse), lambda _: (start // rows, 0))

    taps_two_spec = block(coarse_group, first_rows)
    columns_spec = block(coarse, total_rows - group - coarse)
    taps_one_spec = block(group, total_rows - group)
    there = pl.BlockSpec(memory_space=pl.ANY)

    edge = [
        lax.dynamic_slice_in_dim(image, (rows - SIDE) * half, SIDE, 1).transpose(1, 0, 2),
        lax.dynamic_slice_in_dim(sib, half_rows * half, SIDE, 0),
    ]
    outer = to_outer(jnp.concatenate(edge, axis=1))
    side_shape = ((channels, 2 * LANES), BF16)
    whole, own_sides = call(
        assemble_one_body,
        [((half_rows + 2 * SIDE, channels, LANES), BF16), side_shape],
        name="assemble_one",
    )(own, sib, outer)
    left_in, right_in = sides(own_sides)
    message_rows = 2 * coarse // group

    def scratch_for(wide, high, hid, fetched):
        return [
            pltpu.VMEM((TAPS * TAPS, wide, LANES), BF16),
            pltpu.VMEM((wide, LANES), F32),
            pltpu.VMEM((high + 2 * SIDE, 16, LANES), BF16),
            pltpu.VMEM((high, wide, LANES), BF16),
        ], [
            pltpu.VMEM((2 * hid, 1), F32),
            pltpu.VMEM((wide, 2 * hid), BF16),
            pltpu.VMEM((2, fetched, coarse), BF16),
            pltpu.SemaphoreType.DMA((2,)),
        ]

    before, after = scratch_for(channels, half_rows, hid_one, first_rows)
    block_own, for_sib, pooled, for_outer = call(
        section_one_body,
        [
            ((half_rows, group, LANES), BF16),
            ((half_rows + message_rows, group, LANES), BF16),
            ((packed_rows, coarse, LANES), BF16),
            ((message_rows, group, LANES), BF16),
        ],
        before + [pltpu.VMEM((4, channels, LANES * packed_rows), BF16)] + after,
        flops=10**10,
        moved=10**7,
        name="section_one",
        ins=[None] * 3 + [taps_one_spec] * 2 + [columns_spec] * 2 + [there] * 2,
    )(whole, left_in, right_in, *[packed_own, packed_sib] * 3)
    from_sib = to_sibling(for_sib)
    from_outer = to_outer(for_outer)
    block_came = from_sib[:half_rows]
    side_shape = ((coarse, 2 * LANES), BF16)
    whole_two, own_sides = call(
        assemble_two_body,
        [((packed_rows + 2 * SIDE, coarse, LANES), BF16), side_shape],
        name="assemble_two",
        ins=[
            None,
            pl.BlockSpec((message_rows, group, LANES), lambda _: (half_rows // message_rows, 0, 0)),
            None,
        ],
    )(pooled, from_sib, from_outer)
    left_in, right_in = sides(own_sides)
    block_one = in_order(block_own, block_came).reshape(rows, group, cols).transpose(1, 0, 2)
    whole_two, block_one = lax.optimization_barrier((whole_two, block_one))
    before, after = scratch_for(coarse, packed_rows, hid_two, 2 * hid_two)
    block_shape = ((packed_rows, coarse_group, LANES), BF16)
    two_block_own, two_block_sib = call(
        section_two_body,
        [block_shape, block_shape],
        before + after,
        flops=10**10,
        moved=10**7,
        name="section_two",
        ins=[None] * 3 + [taps_two_spec] * 2 + [columns_spec] * 2 + [there] * 2,
    )(whole_two, left_in, right_in, *[packed_own, packed_sib] * 3)
    two_came = to_sibling(two_block_sib)

    both = in_order(two_block_own, two_came)
    both = both.reshape(2, packed_rows, coarse_group, 2, cols // 2).transpose(2, 0, 3, 1, 4)
    block_two = both.reshape(coarse_group, half_rows, cols // 2)
    return (block_one, block_two)


def solution(mesh):
    tile = P("chan", "row", "col")
    return jax.shard_map(
        on_device,
        mesh=mesh,
        in_specs=(
            tile, P("chan", None, None), P("chan"), P(), P(), P(None, "chan"), P("chan"),
            P("chan", None), P(), P(), P(), P(), P(None, None, "chan"), P("chan"),
            P("chan", None, None), P("chan"), P(), P(), P(None, "chan"), P("chan"),
            P("chan", None), P(), P(),
        ),
        out_specs=(tile, tile),
        check_vma=False,
    )
```
